128 devices in a mesh: dom: 8 (over y, core), bulk: 16 (over x, z).
Axes of the slice: x: 4, y: 4, z: 4, core: 2. Of those that a mesh axis runs over, the one named last changes fastest.
Arguments:
- group_pos: float32 [32768, 3, 128], P(('dom', 'bulk')), may hold values from 0 to 1
- group_vel: float32 [32768, 3, 128], P(('dom', 'bulk')), may hold values from -6 to 6
- leaf_pos: float32 [65536, 3, 128], P(('dom', 'bulk')), may hold values from 0 to 1
- leaf_mass: float32 [65536, 128], P(('dom', 'bulk')), may hold values from 0.0002 to 0.002
- node_pos: float32 [3, 65536], P(None, ('dom', 'bulk')), may hold values from 0 to 1
- node_mass: float32 [65536], P(('dom', 'bulk')), may hold values from 0.002 to 0.02
- group_nodes: int32 [32768, 512], P(('dom', 'bulk')), may hold values from 0 to 511
- export_group: int32 [128, 128, 8], P(('dom', 'bulk')), may hold values from 0 to 255
- export_leaf: int32 [128, 128, 8, 2], P(('dom', 'bulk')), may hold values from 0 to 511
- export_count: int32 [128, 128], P(('dom', 'bulk')), may hold values from 0 to 8, as said below
- move_count: int32 [128], P(('dom', 'bulk')), may hold values from 0 to 16, as said below
Outputs:
- migrated: float32 [34816, 6, 128], P(('dom', 'bulk'))
The draws below stay inside these ranges and needn't reach their ends.
Inputs may be any that keep to these rules, and one draw needn't show every extreme that they name: `export_count`: zero on the diagonal. For each receiver either every other device uses all 8 slots to it, or every sender uses at most 4; at least one receiver is full from every other device. `move_count`: the last device along the curve hands on nothing; some device hands on exactly 16.
All inputs are finite; a program needn't handle non-finite values.
Results may differ from the reference program's by a relative error of at most 0.0003.
Values sent between devices are 32-bit elements; how exact they have to be, the bound alone decides.
No kernel may reach another device: no remote copies, remote signals or barrier semaphores. Data moves between devices by JAX's collectives and lax.ppermute only.
A program may use at most 64 MiB of HBM per device.

```python
import math
import jax
import jax.numpy as jnp
from jax import lax

P_SIZE = 128
G_DEV = 256
L_DEV = 512
NODE_DEV = 512
KN = 512
KL = 2
CAP = 8
MOVE_MAX = 16
GROUPS = 32768
LEAVES = 65536
NODES = 65536
DEVICES = 128


def draw_export_count(key, part):
    key = jax.random.fold_in(key, 11)
    base_key, hot_key, pick_key = jax.random.split(key, 3)
    base = jax.random.randint(base_key, (DEVICES, DEVICES), 0, CAP // 2 + 1)
    hot_flag = jax.random.randint(hot_key, (DEVICES,), 0, 8) == 0
    forced = jax.random.randint(pick_key, (), 0, DEVICES)
    hot_flag = hot_flag | (jnp.arange(DEVICES) == forced)
    counts = jnp.where(hot_flag[None, :], CAP, base)
    diagonal = jnp.arange(DEVICES)[:, None] == jnp.arange(DEVICES)[None, :]
    return jnp.where(diagonal, 0, counts).astype(jnp.int32)


def draw_move_count(key, part):
    key = jax.random.fold_in(key, 23)
    count_key, pick_key = jax.random.split(key, 2)
    counts = jax.random.randint(count_key, (DEVICES,), 0, MOVE_MAX + 1)
    forced = jax.random.randint(pick_key, (), 0, DEVICES - 1)
    counts = jnp.where(jnp.arange(DEVICES) == forced, MOVE_MAX, counts)
    counts = jnp.where(jnp.arange(DEVICES) == DEVICES - 1, 0, counts)
    return counts.astype(jnp.int32)


def with_ends(entries, key, least, largest):
    spot = [jax.random.randint(jax.random.fold_in(key, axis), (), 0, length) for axis, length in enumerate(entries.shape)]
    widest = entries.shape.index(max(entries.shape))
    neighbour = spot[:widest] + [(spot[widest] + 1) % entries.shape[widest]] + spot[widest + 1:]
    return entries.at[tuple(spot)].set(least).at[tuple(neighbour)].set(largest)


def block_scale(stream_key, dims, cuts, least, top_value):
    def one(position, blocks):
        steps = jax.random.uniform(jax.random.fold_in(jax.random.fold_in(stream_key, 6), position), (blocks,), jnp.float32, least / len(cuts), top_value / len(cuts))
        return jnp.repeat(jnp.exp(steps), dims[position] // blocks).reshape((-1,) + (1,) * (len(dims) - position - 1))

    loudness = one(*cuts[0])
    for cut in cuts[1:]:
        loudness = loudness * one(*cut)
    return loudness


def centred(stream_key, dims, width, limit, cuts=(), kind=jnp.bfloat16):
    array = jax.random.normal(stream_key, dims, jnp.float32) * width
    if len(cuts) > 0:
        array = block_scale(stream_key, dims, cuts, -0.22, 0.18) * array
    return jnp.clip(array, min=-limit, max=limit).astype(kind)


def setup_inputs(seed: int = 0) -> dict:
    splits = jax.random.split(jax.random.key(seed), 12)
    return {
        "group_pos": jnp.clip(1.0 * jax.random.uniform(splits[0], (GROUPS, 3, P_SIZE), jnp.float32) ** block_scale(splits[0], (GROUPS, 3, P_SIZE), ((0, 128),), -0.2, 0.2), 0.0, 1.0),
        "group_vel": centred(splits[1], (GROUPS, 3, P_SIZE), 1.0, 6.0, ((0, 128),), jnp.float32),
        "leaf_pos": jnp.clip(1.0 * jax.random.uniform(splits[2], (LEAVES, 3, P_SIZE), jnp.float32) ** block_scale(splits[2], (LEAVES, 3, P_SIZE), ((0, 128),), -0.2, 0.2), 0.0, 1.0),
        "leaf_mass": jnp.clip(jnp.exp(math.log(0.002) - 2.3025852 * jax.random.uniform(splits[3], (LEAVES, P_SIZE), jnp.float32) ** block_scale(splits[3], (LEAVES, P_SIZE), ((0, 128),), -0.2, 0.2)), 0.0002, 0.002),
        "node_pos": jnp.clip(1.0 * jax.random.uniform(splits[4], (3, NODES), jnp.float32) ** block_scale(splits[4], (3, NODES), ((1, 128),), -0.2, 0.2), 0.0, 1.0),
        "node_mass": jnp.clip(jnp.exp(math.log(0.02) - 2.30258502 * jax.random.uniform(splits[5], (NODES,), jnp.float32) ** block_scale(splits[5], (NODES,), ((0, 128),), -0.2, 0.2)), 0.002, 0.02),
        "group_nodes": with_ends(jax.random.randint(splits[6], (GROUPS, KN), 0, NODE_DEV), jax.random.fold_in(splits[6], 1), 0, NODE_DEV - 1).astype(jnp.int32),
        "export_group": with_ends(jax.random.randint(splits[7], (DEVICES, DEVICES, CAP), 0, G_DEV), jax.random.fold_in(splits[7], 1), 0, G_DEV - 1).astype(jnp.int32),
        "export_leaf": with_ends(jax.random.randint(splits[8], (DEVICES, DEVICES, CAP, KL), 0, L_DEV), jax.random.fold_in(splits[8], 1), 0, L_DEV - 1).astype(jnp.int32),
        "export_count": draw_export_count(jax.random.fold_in(splits[11], 71), 0),
        "move_count": draw_move_count(jax.random.fold_in(splits[11], 71), 0),
    }


soft_sq = 0.001
kick_dt = 0.5

def attract(targets, src_pos, src_mass):
    offset = src_pos[:, :, None, :] - targets[:, :, :, None]
    dist_sq = lax.optimization_barrier(jnp.sum(offset * offset, axis=1)) + soft_sq
    weight = src_mass[:, None, :] / (dist_sq * jnp.sqrt(dist_sq))
    return lax.optimization_barrier(jnp.sum(offset * weight[:, None], axis=3))

def blocked_attract(targets, src_pos, src_mass, block_size):
    item_count = targets.shape[0]
    block_size = min(block_size, item_count)
    while item_count % block_size != 0:
        block_size = block_size - 1
    rounds = item_count // block_size

    def one_block(members):
        return attract(members[0], members[1], members[2])
    pieces = (targets.reshape((rounds, block_size) + targets.shape[1:]), src_pos.reshape((rounds, block_size) + src_pos.shape[1:]), src_mass.reshape((rounds, block_size) + src_mass.shape[1:]))
    return lax.map(one_block, pieces).reshape(targets.shape)

def reference(group_pos, group_vel, leaf_pos, leaf_mass, node_pos, node_mass, group_nodes, export_group, export_leaf, export_count, move_count):

    def per_device(device):
        first = device * G_DEV
        own_pos = lax.dynamic_slice_in_dim(group_pos, first, G_DEV, 0)
        own_vel = lax.dynamic_slice_in_dim(group_vel, first, G_DEV, 0)
        near_ids = lax.dynamic_slice_in_dim(group_nodes, first, G_DEV, 0) + device * NODE_DEV
        near_pos = jnp.moveaxis(node_pos[:, near_ids], 0, 1)
        near_mass = node_mass[near_ids]
        local_acc = blocked_attract(own_pos, near_pos, near_mass, 64)
        chosen = export_group[device].reshape(-1)
        leaf_ids = export_leaf[device] + (jnp.arange(DEVICES, dtype=jnp.int32) * L_DEV)[:, None, None]
        aim_pos = own_pos[chosen]
        src_pos = jnp.transpose(leaf_pos[leaf_ids], (0, 1, 3, 2, 4)).reshape(DEVICES * CAP, 3, KL * P_SIZE)
        src_mass = leaf_mass[leaf_ids].reshape(DEVICES * CAP, KL * P_SIZE)
        forces = blocked_attract(aim_pos, src_pos, src_mass, 128)
        usable = (jnp.arange(CAP, dtype=jnp.int32)[None, :] < export_count[device][:, None]).reshape(-1)
        forces = forces * usable.astype(forces.dtype)[:, None, None]
        remote_acc = jax.ops.segment_sum(forces, chosen, num_segments=G_DEV)
        return jnp.concatenate([own_pos, own_vel + kick_dt * (local_acc + remote_acc)], axis=1)
    kicked = lax.map(per_device, jnp.arange(DEVICES, dtype=jnp.int32))
    leaving_rows = kicked[:, G_DEV - MOVE_MAX:]
    arrived = jnp.concatenate([jnp.zeros((1, MOVE_MAX, 6, P_SIZE), kicked.dtype), leaving_rows[:-1]], axis=0)
    before = jnp.concatenate([jnp.zeros((1,), jnp.int32), move_count[:-1].astype(jnp.int32)], axis=0)
    kept_mask = (jnp.arange(G_DEV, dtype=jnp.int32)[None, :] < (G_DEV - move_count)[:, None]).astype(kicked.dtype)
    stacked = jnp.concatenate([arrived, kicked * kept_mask[:, :, None, None], jnp.zeros((DEVICES, MOVE_MAX, 6, P_SIZE), kicked.dtype)], axis=1)

    def place(rows, start):
        return lax.dynamic_slice_in_dim(rows, start, G_DEV + MOVE_MAX, 0)
    moved = jax.vmap(place)(stacked, (MOVE_MAX - before).astype(jnp.int32))
    return moved.reshape(DEVICES * (G_DEV + MOVE_MAX), 6, P_SIZE)
```

```python
import functools

import jax
import jax.numpy as jnp
from jax import lax
from jax.experimental import pallas as pl
from jax.experimental.pallas import tpu as pltpu
from jax.sharding import PartitionSpec as P

AXES = ("dom", "bulk")
MOVE_MAX = 16
SOFT_SQ = 0.001
KICK = 0.5
MID = 0.5
LANES = 128
ROWS = 32

f32 = jnp.float32
bf16 = jnp.bfloat16


def dot(a, b):
    return lax.dot_general(a, b, (((1,), (0,)), ((), ())), preferred_element_type=f32)


def dot_t(a, b):
    return lax.dot_general(a, b, (((1,), (1,)), ((), ())), preferred_element_type=f32)


def split3(v):
    a = v.astype(bf16).astype(f32)
    r = v - a
    b = r.astype(bf16).astype(f32)
    return a, b, r - b


def split2(w):
    hi = w.astype(bf16)
    return hi, (w - hi.astype(f32)).astype(bf16)


def target_rows(x):
    rows = []
    for c in range(3):
        a, b, d = split3(x[c])
        rows += [a, a, b, b, a, d]
    rows += list(split3(x[0] * x[0] + x[1] * x[1] + x[2] * x[2]))
    one = jnp.ones_like(x[0])
    return rows + [one, one, one]


def source_rows(y, scale):
    rows = []
    for c in range(3):
        a, b, d = split3(y[c] * (-2.0 * scale))
        rows += [a, b, a, b, d, a]
    one = jnp.ones_like(y[0]) * scale
    rows += [one, one, one]
    rows += list(split3((y[0] * y[0] + y[1] * y[1] + y[2] * y[2] + SOFT_SQ) * scale))
    return rows


def inv_cube(r2):
    rs = lax.rsqrt(r2)
    return rs * rs * rs


def open_kernel(ids_ref, pos_ref, mass_ref, out_ref, table):
    leaf_count = pos_ref.shape[1]

    def build(b, carry):
        first = pl.multiple_of(b * 8, 8)
        for c in range(4):
            v = pos_ref[c, pl.ds(first, 8), :] if c < 3 else mass_ref[pl.ds(first, 8), :]
            table[pl.ds(first * 8 + c, 8, stride=8), :] = v
            table[pl.ds(first * 8 + 4 + c, 8, stride=8), :] = v
        return carry

    lax.fori_loop(0, leaf_count // 8, build, 0)
    upper = lax.broadcasted_iota(jnp.int32, (8, LANES), 0) < 4

    def one_peer(p, carry):
        for s in range(8):
            i0 = pl.multiple_of(ids_ref[p, 2 * s] * 8, 8)
            i1 = pl.multiple_of(ids_ref[p, 2 * s + 1] * 8, 8)
            out_ref[p, pl.ds(s * 8, 8), :] = jnp.where(
                upper, table[pl.ds(i0, 8), :], table[pl.ds(i1, 8), :]
            )
        return carry

    lax.fori_loop(0, out_ref.shape[0], one_peer, 0)


def open_leaves(ids, leaf_pos, leaf_mass):
    peers = ids.shape[0]
    return pl.pallas_call(
        open_kernel,
        out_shape=jax.ShapeDtypeStruct((peers, 64, LANES), f32),
        in_specs=[
            pl.BlockSpec(memory_space=pltpu.SMEM),
            pl.BlockSpec(memory_space=pltpu.VMEM),
            pl.BlockSpec(memory_space=pltpu.VMEM),
        ],
        out_specs=pl.BlockSpec(memory_space=pltpu.VMEM),
        scratch_shapes=[pltpu.VMEM((leaf_pos.shape[1] * 8, LANES), f32)],
        compiler_params=pltpu.CompilerParams(vmem_limit_bytes=24 << 20),
        name="open_leaves",
    )(ids, leaf_pos, leaf_mass)


def local_kernel(pos_ref, node_ref, mass_ref, list_ref, acc_ref, xt_ref, ynt, xk, raw):
    nodes = node_ref.shape[1]
    y = [node_ref[c : c + 1, :] - MID for c in range(3)]
    mass = mass_ref[...]
    yk = jnp.concatenate(source_rows(y, 1.0) + [jnp.zeros((8, nodes), f32)], axis=0)
    ynt[...] = jnp.transpose(yk).astype(bf16)
    tab = jnp.concatenate([mass * y[0], mass * y[1], mass * y[2], mass], axis=0)
    tab = jnp.concatenate([tab, tab], axis=0)
    xk[...] = jnp.zeros_like(xk)
    row128 = lax.broadcasted_iota(jnp.int32, (LANES, nodes), 0)
    row16 = lax.broadcasted_iota(jnp.int32, (16, nodes), 0)
    eye = (
        lax.broadcasted_iota(jnp.int32, (LANES, LANES), 0)
        == lax.broadcasted_iota(jnp.int32, (LANES, LANES), 1)
    ).astype(f32).astype(bf16)
    upper = lax.broadcasted_iota(jnp.int32, (8, LANES), 0) < 4
    raw[...] = jnp.zeros_like(raw)

    def one_block(b, carry):
        first = pl.multiple_of(b * 8, 8)
        x = [pos_ref[c, pl.ds(first, 8), :] - MID for c in range(3)]
        for r, v in enumerate(target_rows(x)):
            xk[pl.ds(r, 8, stride=ROWS), :] = v
        lists = list_ref[pl.ds(first, 8), :]
        counts = []
        for g in range(8):
            wanted = lists[g : g + 1, :]
            low = jnp.where(row128 == (wanted & 127), 1.0, 0.0).astype(bf16)
            high = jnp.where(row16 == (wanted >> 7), 1.0, 0.0).astype(bf16)
            counts.append(dot_t(high, low))
        for p in range(4):
            parts = []
            for h in range(nodes // LANES):
                both = jnp.where(
                    upper, counts[2 * p][h : h + 1, :], counts[2 * p + 1][h : h + 1, :]
                )
                parts.append(tab[:, h * LANES : (h + 1) * LANES] * both)
            a, d, e = split3(jnp.concatenate(parts, axis=1))
            weights = jnp.concatenate([a, d, e, jnp.zeros_like(a)], axis=0).astype(bf16)
            xa = xk[pl.ds(2 * p * ROWS, ROWS), :]
            xb = xk[pl.ds((2 * p + 1) * ROWS, ROWS), :]
            rhs = jnp.concatenate([xa, xb], axis=1).astype(bf16)
            total = jnp.zeros((32, 2 * LANES), f32)
            for h in range(nodes // 256):
                hi, lo = split2(inv_cube(dot(ynt[pl.ds(h * 256, 256), :], rhs)))
                part = weights[:, h * 256 : (h + 1) * 256]
                total = total + dot(part, hi) + dot(part, lo)
            total = total[0:8] + total[8:16] + total[16:24]
            raw[pl.ds(2 * p * 8, 4), :] = total[0:4, :LANES]
            raw[pl.ds((2 * p + 1) * 8, 4), :] = total[4:8, LANES:]
        weight = raw[pl.ds(3, 8, stride=8), :]
        for c in range(3):
            acc_ref[c, pl.ds(first, 8), :] = raw[pl.ds(c, 8, stride=8), :] - x[c] * weight
        xt = dot_t(eye, xk[...].astype(bf16)).astype(bf16)
        xt_ref[2 * b] = xt[:, :LANES]
        xt_ref[2 * b + 1] = xt[:, LANES:]
        return carry

    lax.fori_loop(0, pos_ref.shape[1] // 8, one_block, 0)


def local_pull(pos, node_pos, node_mass, lists):
    groups = pos.shape[1]
    nodes = node_pos.shape[1]
    pairs = groups * LANES * nodes
    return pl.pallas_call(
        local_kernel,
        out_shape=(
            jax.ShapeDtypeStruct(pos.shape, f32),
            jax.ShapeDtypeStruct((groups // 4, LANES, LANES), bf16),
        ),
        in_specs=[pl.BlockSpec(memory_space=pltpu.VMEM)] * 4,
        out_specs=[pl.BlockSpec(memory_space=pltpu.VMEM)] * 2,
        scratch_shapes=[
            pltpu.VMEM((nodes, ROWS), bf16),
            pltpu.VMEM((8 * ROWS, LANES), f32),
            pltpu.VMEM((64, LANES), f32),
        ],
        compiler_params=pltpu.CompilerParams(vmem_limit_bytes=16 << 20),
        cost_estimate=pl.CostEstimate(
            flops=pairs * 2000, bytes_accessed=4 << 20, transcendentals=pairs
        ),
        name="local_pull",
    )(pos, node_pos, node_mass, lists)


def remote_kernel(
    eg_ref, ec_ref, recv_ref, xt_ref, pos_ref, vel_ref, local_ref, out_ref, todo, xt, tile, yk, tk, acc
):
    peers = ec_ref.shape[0]
    groups = pos_ref.shape[1]

    def unpack(q, carry):
        v = xt_ref[q]
        for j in range(4):
            xt[4 * q + j] = v[:, j * ROWS : (j + 1) * ROWS]
        return carry

    lax.fori_loop(0, groups // 4, unpack, 0)

    def clear(i, carry):
        acc[pl.ds(pl.multiple_of(i * 64, 64), 64), :] = jnp.zeros((64, LANES), f32)
        return carry

    lax.fori_loop(0, groups * 16 // 64, clear, 0)
    yk[...] = jnp.zeros_like(yk)
    tk[...] = jnp.zeros_like(tk)

    def enlist(p, count):
        for s in range(8):
            todo[count + s] = p * 8 + s
        return count + ec_ref[p]

    count = lax.fori_loop(0, peers, enlist, 0)
    for s in range(8):
        todo[count + s] = 0

    lane = lax.broadcasted_iota(jnp.int32, (8, LANES), 1).astype(f32)
    scale = 1.0 + lane * (1.0 / LANES)
    lift = scale * jnp.sqrt(scale)

    def one_block(b, carry):
        slots = []
        for s in range(8):
            k = todo[b * 8 + s]
            slots.append(k)
            tile[pl.ds(s * 8, 8), :] = recv_ref[pl.ds(pl.multiple_of(k * 8, 8), 8), :]
        live = (lax.broadcasted_iota(jnp.int32, (8, LANES), 0) + b * 8) < count
        for h in range(2):
            y = [tile[pl.ds(4 * h + c, 8, stride=8), :] - MID for c in range(3)]
            m = tile[pl.ds(4 * h + 3, 8, stride=8), :]
            m = jnp.where(live, m * lift, 0.0)
            for r, v in enumerate(source_rows(y, scale)):
                yk[pl.ds(h * 8 * ROWS + r, 8, stride=ROWS), :] = v
            for c, v in enumerate([m * y[0], m * y[1], m * y[2], m]):
                for j, part in enumerate(split3(v)):
                    tk[pl.ds(h * 128 + 4 * j + c, 8, stride=16), :] = part
        for s in range(8):
            g = eg_ref[slots[s] & 7, slots[s] >> 3]
            rhs = [yk[pl.ds((h * 8 + s) * ROWS, ROWS), :] for h in range(2)]
            r2 = dot(xt[g], jnp.concatenate(rhs, axis=1).astype(bf16))
            hi, lo = split2(inv_cube(r2))
            part = [tk[pl.ds((h * 8 + s) * 16, 16), :] for h in range(2)]
            part = jnp.concatenate(part, axis=1).astype(bf16)
            rows = pl.ds(pl.multiple_of(g * 16, 16), 16)
            acc[rows, :] += dot_t(part, hi) + dot_t(part, lo)
        return carry

    lax.fori_loop(0, (count + 7) // 8, one_block, 0)

    def finish(b, carry):
        first = pl.multiple_of(b * 8, 8)
        rows = pl.ds(first, 8)
        total = []
        for c in range(4):
            v = acc[pl.ds(first * 16 + c, 8, stride=16), :]
            v = v + acc[pl.ds(first * 16 + 4 + c, 8, stride=16), :]
            total.append(v + acc[pl.ds(first * 16 + 8 + c, 8, stride=16), :])
        for c in range(3):
            x = pos_ref[c, rows, :]
            pull = total[c] - (x - MID) * total[3]
            out_ref[c, rows, :] = x
            out_ref[3 + c, rows, :] = vel_ref[c, rows, :] + KICK * (local_ref[c, rows, :] + pull)
        return carry

    lax.fori_loop(0, groups // 8, finish, 0)


def remote_pull(export_group, export_count, recv, xt, pos, vel, local_acc):
    groups = pos.shape[1]
    peers = export_count.shape[0]
    slots = export_group.shape[0]
    smem = pl.BlockSpec(memory_space=pltpu.SMEM)
    vmem = pl.BlockSpec(memory_space=pltpu.VMEM)
    return pl.pallas_call(
        remote_kernel,
        out_shape=jax.ShapeDtypeStruct((6, groups, LANES), f32),
        in_specs=[smem, smem] + [vmem] * 5,
        out_specs=vmem,
        scratch_shapes=[
            pltpu.SMEM((peers * slots + 8,), jnp.int32),
            pltpu.VMEM((groups, LANES, ROWS), bf16),
            pltpu.VMEM((64, LANES), f32),
            pltpu.VMEM((2 * 8 * ROWS, LANES), f32),
            pltpu.VMEM((2 * 8 * 16, LANES), f32),
            pltpu.VMEM((groups * 16, LANES), f32),
        ],
        compiler_params=pltpu.CompilerParams(vmem_limit_bytes=40 << 20),
        name="remote_pull",
    )(export_group, export_count, recv, xt, pos, vel, local_acc)


def shifted(value, axis, steps):
    count = lax.axis_size(axis)
    return lax.ppermute(value, axis, [(source, source + steps) for source in range(count - steps)])


def per_device(
    group_pos,
    group_vel,
    leaf_pos,
    leaf_mass,
    node_pos,
    node_mass,
    group_nodes,
    export_group,
    export_leaf,
    export_count,
    move_count,
):
    peers = export_group.shape[1]
    groups = group_pos.shape[0]
    before = shifted(move_count, AXES, 1)
    ids = lax.all_to_all(
        export_leaf[0].reshape(peers, 16), AXES, split_axis=0, concat_axis=0, tiled=True
    )
    pos = jnp.transpose(group_pos, (1, 0, 2))
    vel = jnp.transpose(group_vel, (1, 0, 2))
    opened = open_leaves(ids, jnp.transpose(leaf_pos, (1, 0, 2)), leaf_mass)
    recv = lax.all_to_all(opened, AXES, split_axis=0, concat_axis=0, tiled=True)
    local_acc, xt = local_pull(pos, node_pos, node_mass[None, :], group_nodes)
    kicked = remote_pull(
        jnp.transpose(export_group[0]),
        export_count[0],
        recv.reshape(peers * 64, LANES),
        xt,
        pos,
        vel,
        local_acc,
    )
    leaving = move_count[0]
    arrived = shifted(kicked[:, groups - MOVE_MAX :], AXES, 1)
    keep = (jnp.arange(groups) < groups - leaving).astype(f32)
    stacked = jnp.concatenate(
        [arrived, kicked * keep[None, :, None], jnp.zeros((6, MOVE_MAX, LANES), f32)], axis=1
    )
    moved = lax.dynamic_slice_in_dim(stacked, MOVE_MAX - before[0], groups + MOVE_MAX, 1)
    return jnp.transpose(moved, (1, 0, 2))


def solution(mesh):
    in_specs = (
        P(AXES, None, None),
        P(AXES, None, None),
        P(AXES, None, None),
        P(AXES, None),
        P(None, AXES),
        P(AXES),
        P(AXES, None),
        P(AXES, None, None),
        P(AXES, None, None, None),
        P(AXES, None),
        P(AXES),
    )
    return jax.shard_map(
        per_device,
        mesh=mesh,
        in_specs=in_specs,
        out_specs=P(AXES, None, None),
        check_vma=False,
    )
```

```python
import functools

import jax
import jax.numpy as jnp
from jax import lax
from jax.experimental import pallas as pl
from jax.experimental.pallas import tpu as pltpu
from jax.sharding import PartitionSpec as P

AXES = ("dom", "bulk")
MOVE_MAX = 16
SOFT_SQ = 0.001
KICK = 0.5
MID = 0.5
LANES = 128
ROWS = 32

f32 = jnp.float32
bf16 = jnp.bfloat16


def dot(a, b):
    return lax.dot_general(a, b, (((1,), (0,)), ((), ())), preferred_element_type=f32)


def dot_t(a, b):
    return lax.dot_general(a, b, (((1,), (1,)), ((), ())), preferred_element_type=f32)


def split3(v):
    a = v.astype(bf16).astype(f32)
    r = v - a
    b = r.astype(bf16).astype(f32)
    return a, b, r - b


def split2(w):
    hi = w.astype(bf16)
    return hi, (w - hi.astype(f32)).astype(bf16)


def target_rows(x):
    rows = []
    for c in range(3):
        a, b, d = split3(x[c])
        rows += [a, a, b, b, a, d]
    rows += list(split3(x[0] * x[0] + x[1] * x[1] + x[2] * x[2]))
    one = jnp.ones_like(x[0])
    return rows + [one, one, one]


def source_rows(y, scale):
    rows = []
    for c in range(3):
        a, b, d = split3(y[c] * (-2.0 * scale))
        rows += [a, b, a, b, d, a]
    one = jnp.ones_like(y[0]) * scale
    rows += [one, one, one]
    rows += list(split3((y[0] * y[0] + y[1] * y[1] + y[2] * y[2] + SOFT_SQ) * scale))
    return rows


def inv_cube(r2):
    rs = lax.rsqrt(r2)
    return rs * rs * rs


def open_kernel(ids_ref, pos_ref, mass_ref, out_ref, table):
    leaf_count = pos_ref.shape[1]

    def build(b, carry):
        first = pl.multiple_of(b * 8, 8)
        for c in range(4):
            v = pos_ref[c, pl.ds(first, 8), :] if c < 3 else mass_ref[pl.ds(first, 8), :]
            table[pl.ds(first * 8 + c, 8, stride=8), :] = v
            table[pl.ds(first * 8 + 4 + c, 8, stride=8), :] = v
        return carry

    lax.fori_loop(0, leaf_count // 8, build, 0)
    upper = lax.broadcasted_iota(jnp.int32, (8, LANES), 0) < 4

    def one_peer(p, carry):
        for s in range(8):
            i0 = pl.multiple_of(ids_ref[p, 2 * s] * 8, 8)
            i1 = pl.multiple_of(ids_ref[p, 2 * s + 1] * 8, 8)
            out_ref[p, pl.ds(s * 8, 8), :] = jnp.where(
                upper, table[pl.ds(i0, 8), :], table[pl.ds(i1, 8), :]
            )
        return carry

    lax.fori_loop(0, out_ref.shape[0], one_peer, 0)


def open_leaves(ids, leaf_pos, leaf_mass):
    peers = ids.shape[0]
    return pl.pallas_call(
        open_kernel,
        out_shape=jax.ShapeDtypeStruct((peers, 64, LANES), f32),
        in_specs=[
            pl.BlockSpec(memory_space=pltpu.SMEM),
            pl.BlockSpec(memory_space=pltpu.VMEM),
            pl.BlockSpec(memory_space=pltpu.VMEM),
        ],
        out_specs=pl.BlockSpec(memory_space=pltpu.VMEM),
        scratch_shapes=[pltpu.VMEM((leaf_pos.shape[1] * 8, LANES), f32)],
        compiler_params=pltpu.CompilerParams(vmem_limit_bytes=24 << 20),
        name="open_leaves",
    )(ids, leaf_pos, leaf_mass)


def local_kernel(begin, pos_ref, node_ref, mass_ref, list_ref, acc_ref, xt_ref, ynt, xk, raw):
    nodes = node_ref.shape[1]
    y = [node_ref[c : c + 1, :] - MID for c in range(3)]
    mass = mass_ref[...]
    yk = jnp.concatenate(source_rows(y, 1.0) + [jnp.zeros((8, nodes), f32)], axis=0)
    ynt[...] = jnp.transpose(yk).astype(bf16)
    tab = jnp.concatenate([mass * y[0], mass * y[1], mass * y[2], mass], axis=0)
    tab = jnp.concatenate([tab, tab], axis=0)
    xk[...] = jnp.zeros_like(xk)
    row128 = lax.broadcasted_iota(jnp.int32, (LANES, nodes), 0)
    row16 = lax.broadcasted_iota(jnp.int32, (16, nodes), 0)
    eye = (
        lax.broadcasted_iota(jnp.int32, (LANES, LANES), 0)
        == lax.broadcasted_iota(jnp.int32, (LANES, LANES), 1)
    ).astype(f32).astype(bf16)
    upper = lax.broadcasted_iota(jnp.int32, (8, LANES), 0) < 4
    raw[...] = jnp.zeros_like(raw)

    def one_block(b, carry):
        first = pl.multiple_of(b * 8, 8)
        place = pl.multiple_of(begin + b * 8, 8)
        x = [pos_ref[c, pl.ds(place, 8), :] - MID for c in range(3)]
        for r, v in enumerate(target_rows(x)):
            xk[pl.ds(r, 8, stride=ROWS), :] = v
        lists = list_ref[pl.ds(place, 8), :]
        counts = []
        for g in range(8):
            wanted = lists[g : g + 1, :]
            low = jnp.where(row128 == (wanted & 127), 1.0, 0.0).astype(bf16)
            high = jnp.where(row16 == (wanted >> 7), 1.0, 0.0).astype(bf16)
            counts.append(dot_t(high, low))
        for p in range(4):
            parts = []
            for h in range(nodes // LANES):
                both = jnp.where(
                    upper, counts[2 * p][h : h + 1, :], counts[2 * p + 1][h : h + 1, :]
                )
                parts.append(tab[:, h * LANES : (h + 1) * LANES] * both)
            a, d, e = split3(jnp.concatenate(parts, axis=1))
            weights = jnp.concatenate([a, d, e, jnp.zeros_like(a)], axis=0).astype(bf16)
            xa = xk[pl.ds(2 * p * ROWS, ROWS), :]
            xb = xk[pl.ds((2 * p + 1) * ROWS, ROWS), :]
            rhs = jnp.concatenate([xa, xb], axis=1).astype(bf16)
            total = jnp.zeros((32, 2 * LANES), f32)
            for h in range(nodes // 256):
                hi, lo = split2(inv_cube(dot(ynt[pl.ds(h * 256, 256), :], rhs)))
                part = weights[:, h * 256 : (h + 1) * 256]
                total = total + dot(part, hi) + dot(part, lo)
            total = total[0:8] + total[8:16] + total[16:24]
            raw[pl.ds(2 * p * 8, 4), :] = total[0:4, :LANES]
            raw[pl.ds((2 * p + 1) * 8, 4), :] = total[4:8, LANES:]
        weight = raw[pl.ds(3, 8, stride=8), :]
        for c in range(3):
            acc_ref[c, pl.ds(first, 8), :] = raw[pl.ds(c, 8, stride=8), :] - x[c] * weight
        xt = dot_t(eye, xk[...].astype(bf16)).astype(bf16)
        xt_ref[2 * b] = xt[:, :LANES]
        xt_ref[2 * b + 1] = xt[:, LANES:]
        return carry

    lax.fori_loop(0, acc_ref.shape[1] // 8, one_block, 0)


def local_pull(pos, node_pos, node_mass, lists, begin, end):
    groups = end - begin
    nodes = node_pos.shape[1]
    pairs = groups * LANES * nodes
    return pl.pallas_call(
        functools.partial(local_kernel, begin),
        out_shape=(
            jax.ShapeDtypeStruct((3, groups, LANES), f32),
            jax.ShapeDtypeStruct((groups // 4, LANES, LANES), bf16),
        ),
        in_specs=[pl.BlockSpec(memory_space=pltpu.VMEM)] * 4,
        out_specs=[pl.BlockSpec(memory_space=pltpu.VMEM)] * 2,
        scratch_shapes=[
            pltpu.VMEM((nodes, ROWS), bf16),
            pltpu.VMEM((8 * ROWS, LANES), f32),
            pltpu.VMEM((64, LANES), f32),
        ],
        compiler_params=pltpu.CompilerParams(vmem_limit_bytes=16 << 20),
        cost_estimate=pl.CostEstimate(
            flops=pairs * 2000, bytes_accessed=4 << 20, transcendentals=pairs
        ),
        name="local_pull",
    )(pos, node_pos, node_mass, lists)


def remote_kernel(
    eg_ref,
    ec_ref,
    recv_ref,
    xt0_ref,
    xt1_ref,
    pos_ref,
    vel_ref,
    local0_ref,
    local1_ref,
    out_ref,
    todo,
    xt,
    tile,
    yk,
    tk,
    acc,
):
    peers = ec_ref.shape[0]
    groups = pos_ref.shape[1]

    def unpack(ref, base, q, carry):
        for i in range(4):
            v = ref[4 * q + i]
            for j in range(4):
                xt[base + 16 * q + 4 * i + j] = v[:, j * ROWS : (j + 1) * ROWS]
        return carry

    early = local0_ref.shape[1]
    lax.fori_loop(0, early // 16, functools.partial(unpack, xt0_ref, 0), 0)
    lax.fori_loop(0, (groups - early) // 16, functools.partial(unpack, xt1_ref, early), 0)

    def clear(i, carry):
        acc[pl.ds(pl.multiple_of(i * 64, 64), 64), :] = jnp.zeros((64, LANES), f32)
        return carry

    lax.fori_loop(0, groups * 16 // 64, clear, 0)
    yk[...] = jnp.zeros_like(yk)
    tk[...] = jnp.zeros_like(tk)

    def enlist(p, count):
        for s in range(8):
            todo[count + s] = p * 8 + s
        return count + ec_ref[p]

    count = lax.fori_loop(0, peers, enlist, 0)
    for s in range(8):
        todo[count + s] = 0

    lane = lax.broadcasted_iota(jnp.int32, (8, LANES), 1).astype(f32)
    scale = 1.0 + lane * (1.0 / LANES)
    lift = scale * jnp.sqrt(scale)

    def one_block(b, carry):
        slots = []
        for s in range(8):
            k = todo[b * 8 + s]
            slots.append(k)
            tile[pl.ds(s * 8, 8), :] = recv_ref[pl.ds(pl.multiple_of(k * 8, 8), 8), :]
        live = (lax.broadcasted_iota(jnp.int32, (8, LANES), 0) + b * 8) < count
        for h in range(2):
            y = [tile[pl.ds(4 * h + c, 8, stride=8), :] - MID for c in range(3)]
            m = tile[pl.ds(4 * h + 3, 8, stride=8), :]
            m = jnp.where(live, m * lift, 0.0)
            for r, v in enumerate(source_rows(y, scale)):
                yk[pl.ds(h * 8 * ROWS + r, 8, stride=ROWS), :] = v
            for c, v in enumerate([m * y[0], m * y[1], m * y[2], m]):
                for j, part in enumerate(split3(v)):
                    tk[pl.ds(h * 128 + 4 * j + c, 8, stride=16), :] = part
        for s in range(8):
            g = eg_ref[slots[s] & 7, slots[s] >> 3]
            rhs = [yk[pl.ds((h * 8 + s) * ROWS, ROWS), :] for h in range(2)]
            r2 = dot(xt[g], jnp.concatenate(rhs, axis=1).astype(bf16))
            part = [tk[pl.ds((h * 8 + s) * 16, 16), :] for h in range(2)]
            part = jnp.concatenate(part, axis=1).astype(bf16)
            rows = pl.ds(pl.multiple_of(g * 16, 16), 16)
            acc[rows, :] += dot_t(part, inv_cube(r2).astype(bf16))
        return carry

    lax.fori_loop(0, (count + 7) // 8, one_block, 0)

    def finish(ref, base, b, carry):
        first = pl.multiple_of(base + b * 8, 8)
        rows = pl.ds(first, 8)
        near = pl.ds(pl.multiple_of(b * 8, 8), 8)
        total = []
        for c in range(4):
            v = acc[pl.ds(first * 16 + c, 8, stride=16), :]
            v = v + acc[pl.ds(first * 16 + 4 + c, 8, stride=16), :]
            total.append(v + acc[pl.ds(first * 16 + 8 + c, 8, stride=16), :])
        for c in range(3):
            x = pos_ref[c, rows, :]
            pull = total[c] - (x - MID) * total[3]
            out_ref[c, rows, :] = x
            out_ref[3 + c, rows, :] = vel_ref[c, rows, :] + KICK * (ref[c, near, :] + pull)
        return carry

    lax.fori_loop(0, early // 8, functools.partial(finish, local0_ref, 0), 0)
    lax.fori_loop(0, (groups - early) // 8, functools.partial(finish, local1_ref, early), 0)


def remote_pull(export_group, export_count, recv, pos, vel, near0, near1):
    groups = pos.shape[1]
    peers = export_count.shape[0]
    slots = export_group.shape[0]
    smem = pl.BlockSpec(memory_space=pltpu.SMEM)
    vmem = pl.BlockSpec(memory_space=pltpu.VMEM)
    return pl.pallas_call(
        remote_kernel,
        out_shape=jax.ShapeDtypeStruct((6, groups, LANES), f32),
        in_specs=[smem, smem] + [vmem] * 7,
        out_specs=vmem,
        scratch_shapes=[
            pltpu.SMEM((peers * slots + 8,), jnp.int32),
            pltpu.VMEM((groups, LANES, ROWS), bf16),
            pltpu.VMEM((64, LANES), f32),
            pltpu.VMEM((2 * 8 * ROWS, LANES), f32),
            pltpu.VMEM((2 * 8 * 16, LANES), f32),
            pltpu.VMEM((groups * 16, LANES), f32),
        ],
        compiler_params=pltpu.CompilerParams(vmem_limit_bytes=40 << 20),
        name="remote_pull",
    )(export_group, export_count, recv, near0[1], near1[1], pos, vel, near0[0], near1[0])


def shifted(value, axis, steps):
    count = lax.axis_size(axis)
    return lax.ppermute(value, axis, [(source, source + steps) for source in range(count - steps)])


def per_device(
    group_pos,
    group_vel,
    leaf_pos,
    leaf_mass,
    node_pos,
    node_mass,
    group_nodes,
    export_group,
    export_leaf,
    export_count,
    move_count,
):
    peers = export_group.shape[1]
    groups = group_pos.shape[0]
    early = groups * 3 // 16
    asked = jnp.concatenate(
        [export_leaf[0].reshape(peers, 16), jnp.broadcast_to(move_count[:, None], (peers, 1))], axis=1
    )
    got = lax.all_to_all(asked, AXES, split_axis=0, concat_axis=0, tiled=True)
    pos = jnp.transpose(group_pos, (1, 0, 2))
    vel = jnp.transpose(group_vel, (1, 0, 2))
    mass = node_mass[None, :]
    near0 = local_pull(pos, node_pos, mass, group_nodes, 0, early)
    got, near0 = lax.optimization_barrier((got, near0))
    opened = open_leaves(got, jnp.transpose(leaf_pos, (1, 0, 2)), leaf_mass)
    opened, mass = lax.optimization_barrier((opened, mass))
    recv = lax.all_to_all(opened, AXES, split_axis=0, concat_axis=0, tiled=True)
    near1 = local_pull(pos, node_pos, mass, group_nodes, early, groups)
    kicked = remote_pull(
        jnp.transpose(export_group[0]),
        export_count[0],
        recv.reshape(peers * 64, LANES),
        pos,
        vel,
        near0,
        near1,
    )
    me = lax.axis_index(AXES)
    before = jnp.where(me > 0, got[jnp.maximum(me - 1, 0), 16], 0)
    leaving = move_count[0]
    arrived = shifted(kicked[:, groups - MOVE_MAX :], AXES, 1)
    keep = (jnp.arange(groups) < groups - leaving).astype(f32)
    stacked = jnp.concatenate(
        [arrived, kicked * keep[None, :, None], jnp.zeros((6, MOVE_MAX, LANES), f32)], axis=1
    )
    moved = lax.dynamic_slice_in_dim(stacked, MOVE_MAX - before, groups + MOVE_MAX, 1)
    return jnp.transpose(moved, (1, 0, 2))


def solution(mesh):
    in_specs = (
        P(AXES, None, None),
        P(AXES, None, None),
        P(AXES, None, None),
        P(AXES, None),
        P(None, AXES),
        P(AXES),
        P(AXES, None),
        P(AXES, None, None),
        P(AXES, None, None, None),
        P(AXES, None),
        P(AXES),
    )
    return jax.shard_map(
        per_device,
        mesh=mesh,
        in_specs=in_specs,
        out_specs=P(AXES, None, None),
        check_vma=False,
    )
```

```python
import functools

import jax
import jax.numpy as jnp
from jax import lax
from jax.experimental import pallas as pl
from jax.experimental.pallas import tpu as pltpu
from jax.sharding import PartitionSpec as P

AXES = ("dom", "bulk")
MOVE_MAX = 16
SOFT_SQ = 0.001
KICK = 0.5
MID = 0.5
LANES = 128
ROWS = 32
SPAN = 4

f32 = jnp.float32
bf16 = jnp.bfloat16


def dot(a, b):
    return lax.dot_general(a, b, (((1,), (0,)), ((), ())), preferred_element_type=f32)


def dot_t(a, b):
    return lax.dot_general(a, b, (((1,), (1,)), ((), ())), preferred_element_type=f32)


def split3(v):
    a = v.astype(bf16).astype(f32)
    r = v - a
    b = r.astype(bf16).astype(f32)
    return a, b, r - b


def split2(w):
    hi = w.astype(bf16)
    return hi, (w - hi.astype(f32)).astype(bf16)


def target_rows(x):
    rows = []
    for c in range(3):
        a, b, d = split3(x[c])
        rows += [a, a, b, b, a, d]
    rows += list(split3(x[0] * x[0] + x[1] * x[1] + x[2] * x[2]))
    one = jnp.ones_like(x[0])
    return rows + [one, one, one]


def source_rows(y, scale):
    rows = []
    for c in range(3):
        a, b, d = split3(y[c] * (-2.0 * scale))
        rows += [a, b, a, b, d, a]
    one = jnp.ones_like(y[0]) * scale
    rows += [one, one, one]
    rows += list(split3((y[0] * y[0] + y[1] * y[1] + y[2] * y[2] + SOFT_SQ) * scale))
    return rows


def inv_cube(r2):
    rs = lax.rsqrt(r2)
    return rs * rs * rs


def open_kernel(base, ids_ref, pos_ref, mass_ref, out_ref, table):
    leaf_count = pos_ref.shape[1]

    def build(b, carry):
        first = pl.multiple_of(b * 8, 8)
        for c in range(4):
            v = pos_ref[c, pl.ds(first, 8), :] if c < 3 else mass_ref[pl.ds(first, 8), :]
            table[pl.ds(first * 8 + c, 8, stride=8), :] = v
            table[pl.ds(first * 8 + 4 + c, 8, stride=8), :] = v
        return carry

    lax.fori_loop(0, leaf_count // 8, build, 0, unroll=4)
    upper = lax.broadcasted_iota(jnp.int32, (8, LANES), 0) < 4

    def one_peer(p, carry):
        for s in range(SPAN):
            i0 = pl.multiple_of(ids_ref[p, 2 * (base + s)] * 8, 8)
            i1 = pl.multiple_of(ids_ref[p, 2 * (base + s) + 1] * 8, 8)
            out_ref[p, pl.ds(s * 8, 8), :] = jnp.where(
                upper, table[pl.ds(i0, 8), :], table[pl.ds(i1, 8), :]
            )
        return carry

    lax.fori_loop(0, out_ref.shape[0], one_peer, 0, unroll=4)


def open_leaves(ids, leaf_pos, leaf_mass, base):
    peers = ids.shape[0]
    return pl.pallas_call(
        functools.partial(open_kernel, base),
        out_shape=jax.ShapeDtypeStruct((peers, SPAN * 8, LANES), f32),
        in_specs=[
            pl.BlockSpec(memory_space=pltpu.SMEM),
            pl.BlockSpec(memory_space=pltpu.VMEM),
            pl.BlockSpec(memory_space=pltpu.VMEM),
        ],
        out_specs=pl.BlockSpec(memory_space=pltpu.VMEM),
        scratch_shapes=[pltpu.VMEM((leaf_pos.shape[1] * 8, LANES), f32)],
        compiler_params=pltpu.CompilerParams(vmem_limit_bytes=12 << 20),
        name="open_leaves",
    )(ids, leaf_pos, leaf_mass)


def local_kernel(begin, emit, pos_ref, node_ref, mass_ref, list_ref, acc_ref, *rest):
    xt_ref = rest[0] if emit else None
    ynt, xk, raw = rest[-3:]
    nodes = node_ref.shape[1]
    y = [node_ref[c : c + 1, :] - MID for c in range(3)]
    mass = mass_ref[...]
    yk = jnp.concatenate(source_rows(y, 1.0) + [jnp.zeros((8, nodes), f32)], axis=0)
    ynt[...] = jnp.transpose(yk).astype(bf16)
    tab = jnp.concatenate([mass * y[0], mass * y[1], mass * y[2], mass], axis=0)
    tab = jnp.concatenate([tab, tab], axis=0)
    xk[...] = jnp.zeros_like(xk)
    row128 = lax.broadcasted_iota(jnp.int32, (LANES, nodes), 0)
    row16 = lax.broadcasted_iota(jnp.int32, (16, nodes), 0)
    upper = lax.broadcasted_iota(jnp.int32, (8, LANES), 0) < 4
    raw[...] = jnp.zeros_like(raw)

    def stage(place):
        x = [pos_ref[c, pl.ds(place, 8), :] - MID for c in range(3)]
        for r, v in enumerate(target_rows(x)):
            xk[pl.ds(r, 8, stride=ROWS), :] = v
        if emit:
            for g in range(8):
                xt_ref[place + g] = jnp.transpose(xk[pl.ds(g * ROWS, ROWS), :]).astype(bf16)
        return x

    def only_stage(b, carry):
        stage(pl.multiple_of(b * 8, 8))
        return carry

    if emit:
        lax.fori_loop(0, begin // 8, only_stage, 0)

    def one_block(b, carry):
        first = pl.multiple_of(b * 8, 8)
        place = pl.multiple_of(begin + b * 8, 8)
        x = stage(place)
        lists = list_ref[pl.ds(place, 8), :]
        counts = []
        for g in range(8):
            wanted = lists[g : g + 1, :]
            low = jnp.where(row128 == (wanted & 127), 1.0, 0.0).astype(bf16)
            high = jnp.where(row16 == (wanted >> 7), 1.0, 0.0).astype(bf16)
            counts.append(dot_t(high, low))
        for p in range(4):
            parts = []
            for h in range(nodes // LANES):
                both = jnp.where(
                    upper, counts[2 * p][h : h + 1, :], counts[2 * p + 1][h : h + 1, :]
                )
                parts.append(tab[:, h * LANES : (h + 1) * LANES] * both)
            a, d, e = split3(jnp.concatenate(parts, axis=1))
            weights = jnp.concatenate([a, d, e, jnp.zeros_like(a)], axis=0).astype(bf16)
            xa = xk[pl.ds(2 * p * ROWS, ROWS), :]
            xb = xk[pl.ds((2 * p + 1) * ROWS, ROWS), :]
            rhs = jnp.concatenate([xa, xb], axis=1).astype(bf16)
            total = jnp.zeros((32, 2 * LANES), f32)
            for h in range(nodes // 256):
                his, los = [], []
                for k in range(256 // 128):
                    rows = pl.ds(h * 256 + k * 128, 128)
                    a, d = split2(inv_cube(dot(ynt[rows, :], rhs)))
                    his.append(a)
                    los.append(d)
                part = weights[:, h * 256 : (h + 1) * 256]
                total = total + dot(part, jnp.concatenate(his, axis=0)) + dot(part, jnp.concatenate(los, axis=0))
            total = total[0:8] + total[8:16] + total[16:24]
            raw[pl.ds(2 * p * 8, 4), :] = total[0:4, :LANES]
            raw[pl.ds((2 * p + 1) * 8, 4), :] = total[4:8, LANES:]
        weight = raw[pl.ds(3, 8, stride=8), :]
        for c in range(3):
            acc_ref[c, pl.ds(first, 8), :] = raw[pl.ds(c, 8, stride=8), :] - x[c] * weight
        return carry

    lax.fori_loop(0, acc_ref.shape[1] // 8, one_block, 0)


def local_pull(pos, node_pos, node_mass, lists, begin, end, emit):
    groups = end - begin
    nodes = node_pos.shape[1]
    pairs = groups * LANES * nodes
    out_shape = [jax.ShapeDtypeStruct((3, groups, LANES), f32)]
    if emit:
        out_shape.append(jax.ShapeDtypeStruct((pos.shape[1], LANES, ROWS), bf16))
    return pl.pallas_call(
        functools.partial(local_kernel, begin, emit),
        out_shape=out_shape,
        in_specs=[pl.BlockSpec(memory_space=pltpu.VMEM)] * 4,
        out_specs=[pl.BlockSpec(memory_space=pltpu.VMEM)] * len(out_shape),
        scratch_shapes=[
            pltpu.VMEM((nodes, ROWS), bf16),
            pltpu.VMEM((8 * ROWS, LANES), f32),
            pltpu.VMEM((64, LANES), f32),
        ],
        compiler_params=pltpu.CompilerParams(vmem_limit_bytes=16 << 20),
        cost_estimate=pl.CostEstimate(
            flops=pairs * 2000, bytes_accessed=4 << 20, transcendentals=pairs
        ),
        name="local_pull",
    )(pos, node_pos, node_mass, lists)


def exported_pull(base, eg_ref, ec_ref, recv_ref, xt_ref, acc, todo, tile, yk, tk):
    yk[...] = jnp.zeros_like(yk)
    tk[...] = jnp.zeros_like(tk)

    def enlist(p, count):
        for s in range(SPAN):
            todo[count + s] = p * SPAN + s
        return count + jnp.clip(ec_ref[p] - base, 0, SPAN)

    count = lax.fori_loop(0, ec_ref.shape[0], enlist, 0, unroll=4)
    for s in range(8):
        todo[count + s] = 0

    lane = lax.broadcasted_iota(jnp.int32, (8, LANES), 1).astype(f32)
    scale = 1.0 + lane * (1.0 / LANES)
    lift = scale * jnp.sqrt(scale)

    def one_block(b, carry):
        slots = []
        for s in range(8):
            k = todo[b * 8 + s]
            slots.append(k)
            tile[pl.ds(s * 8, 8), :] = recv_ref[pl.ds(pl.multiple_of(k * 8, 8), 8), :]
        live = (lax.broadcasted_iota(jnp.int32, (8, LANES), 0) + b * 8) < count
        for h in range(2):
            y = [tile[pl.ds(4 * h + c, 8, stride=8), :] - MID for c in range(3)]
            m = tile[pl.ds(4 * h + 3, 8, stride=8), :]
            m = jnp.where(live, m * lift, 0.0)
            for r, v in enumerate(source_rows(y, scale)):
                yk[pl.ds(h * 8 * ROWS + r, 8, stride=ROWS), :] = v
            for c, v in enumerate([m * y[0], m * y[1], m * y[2], m]):
                for j, part in enumerate(split3(v)):
                    tk[pl.ds(h * 128 + 4 * j + c, 8, stride=16), :] = part
        for s in range(8):
            g = eg_ref[base + lax.rem(slots[s], SPAN), lax.div(slots[s], SPAN)]
            rhs = [yk[pl.ds((h * 8 + s) * ROWS, ROWS), :] for h in range(2)]
            r2 = dot(xt_ref[g], jnp.concatenate(rhs, axis=1).astype(bf16))
            part = [tk[pl.ds((h * 8 + s) * 16, 16), :] for h in range(2)]
            part = jnp.concatenate(part, axis=1).astype(bf16)
            rows = pl.ds(pl.multiple_of(g * 16, 16), 16)
            acc[rows, :] += dot_t(part, inv_cube(r2).astype(bf16))
        return carry

    lax.fori_loop(0, (count + 7) // 8, one_block, 0)


def first_kernel(eg_ref, ec_ref, recv_ref, xt_ref, acc_ref, todo, tile, yk, tk):
    def clear(i, carry):
        acc_ref[pl.ds(pl.multiple_of(i * 64, 64), 64), :] = jnp.zeros((64, LANES), f32)
        return carry

    lax.fori_loop(0, acc_ref.shape[0] // 64, clear, 0)
    exported_pull(0, eg_ref, ec_ref, recv_ref, xt_ref, acc_ref, todo, tile, yk, tk)


def last_kernel(
    eg_ref,
    ec_ref,
    recv_ref,
    xt_ref,
    old_ref,
    pos_ref,
    vel_ref,
    local0_ref,
    local1_ref,
    out_ref,
    acc_ref,
    todo,
    tile,
    yk,
    tk,
):
    exported_pull(SPAN, eg_ref, ec_ref, recv_ref, xt_ref, acc_ref, todo, tile, yk, tk)
    groups = pos_ref.shape[1]
    early = local0_ref.shape[1]

    def finish(ref, base, b, carry):
        first = pl.multiple_of(base + b * 8, 8)
        rows = pl.ds(first, 8)
        near = pl.ds(pl.multiple_of(b * 8, 8), 8)
        total = []
        for c in range(4):
            v = acc_ref[pl.ds(first * 16 + c, 8, stride=16), :]
            v = v + acc_ref[pl.ds(first * 16 + 4 + c, 8, stride=16), :]
            total.append(v + acc_ref[pl.ds(first * 16 + 8 + c, 8, stride=16), :])
        for c in range(3):
            x = pos_ref[c, rows, :]
            pull = total[c] - (x - MID) * total[3]
            out_ref[c, rows, :] = x
            out_ref[3 + c, rows, :] = vel_ref[c, rows, :] + KICK * (ref[c, near, :] + pull)
        return carry

    lax.fori_loop(0, early // 8, functools.partial(finish, local0_ref, 0), 0)
    lax.fori_loop(0, (groups - early) // 8, functools.partial(finish, local1_ref, early), 0)


def exported_scratch(slots):
    return [
        pltpu.SMEM((slots + 8,), jnp.int32),
        pltpu.VMEM((64, LANES), f32),
        pltpu.VMEM((2 * 8 * ROWS, LANES), f32),
        pltpu.VMEM((2 * 8 * 16, LANES), f32),
    ]


SMEM_SPEC = pl.BlockSpec(memory_space=pltpu.SMEM)
VMEM_SPEC = pl.BlockSpec(memory_space=pltpu.VMEM)


def first_pull(export_group, export_count, recv, xt):
    slots, peers = export_group.shape
    return pl.pallas_call(
        first_kernel,
        out_shape=jax.ShapeDtypeStruct((xt.shape[0] * 16, LANES), f32),
        in_specs=[SMEM_SPEC] * 2 + [VMEM_SPEC] * 2,
        out_specs=VMEM_SPEC,
        scratch_shapes=exported_scratch(peers * SPAN),
        compiler_params=pltpu.CompilerParams(vmem_limit_bytes=24 << 20),
        cost_estimate=pl.CostEstimate(
            flops=peers * SPAN * 65536000, bytes_accessed=4 << 20, transcendentals=0
        ),
        name="first_pull",
    )(export_group, export_count, recv, xt)


def last_pull(export_group, export_count, recv, xt, acc, pos, vel, local0, local1):
    slots, peers = export_group.shape
    return pl.pallas_call(
        last_kernel,
        out_shape=(
            jax.ShapeDtypeStruct((6,) + pos.shape[1:], f32),
            jax.ShapeDtypeStruct(acc.shape, f32),
        ),
        in_specs=[SMEM_SPEC] * 2 + [VMEM_SPEC] * 7,
        out_specs=[VMEM_SPEC] * 2,
        scratch_shapes=exported_scratch(peers * SPAN),
        input_output_aliases={4: 1},
        compiler_params=pltpu.CompilerParams(vmem_limit_bytes=24 << 20),
        name="last_pull",
    )(export_group, export_count, recv, xt, acc, pos, vel, local0, local1)[0]


def shifted(value, axis, steps):
    count = lax.axis_size(axis)
    return lax.ppermute(value, axis, [(source, source + steps) for source in range(count - steps)])


def per_device(
    group_pos,
    group_vel,
    leaf_pos,
    leaf_mass,
    node_pos,
    node_mass,
    group_nodes,
    export_group,
    export_leaf,
    export_count,
    move_count,
):
    peers = export_group.shape[1]
    groups = group_pos.shape[0]
    early = groups * 3 // 16
    asked = jnp.concatenate(
        [export_leaf[0].reshape(peers, 16), jnp.broadcast_to(move_count[:, None], (peers, 1))], axis=1
    )
    got = lax.all_to_all(asked, AXES, split_axis=0, concat_axis=0, tiled=True)
    pos = jnp.transpose(group_pos, (1, 0, 2))
    vel = jnp.transpose(group_vel, (1, 0, 2))
    mass = node_mass[None, :]
    (local0,) = local_pull(pos, node_pos, mass, group_nodes, 0, early, False)
    got, local0 = lax.optimization_barrier((got, local0))
    leaf = jnp.transpose(leaf_pos, (1, 0, 2))
    opened = open_leaves(got, leaf, leaf_mass, 0)
    opened, mass = lax.optimization_barrier((opened, mass))
    recv = lax.all_to_all(opened, AXES, split_axis=0, concat_axis=0, tiled=True)
    local1, xt = local_pull(pos, node_pos, mass, group_nodes, early, groups, True)
    got2, recv, local1, xt = lax.optimization_barrier((got, recv, local1, xt))
    opened2 = open_leaves(got2, leaf, leaf_mass, SPAN)
    opened2, recv = lax.optimization_barrier((opened2, recv))
    recv2 = lax.all_to_all(opened2, AXES, split_axis=0, concat_axis=0, tiled=True)
    exported = jnp.transpose(export_group[0])
    acc = first_pull(exported, export_count[0], recv.reshape(-1, LANES), xt)
    kicked = last_pull(
        exported, export_count[0], recv2.reshape(-1, LANES), xt, acc, pos, vel, local0, local1
    )
    me = lax.axis_index(AXES)
    before = jnp.where(me > 0, got[jnp.maximum(me - 1, 0), 16], 0)
    leaving = move_count[0]
    arrived = shifted(kicked[:, groups - MOVE_MAX :], AXES, 1)
    keep = (jnp.arange(groups) < groups - leaving).astype(f32)
    stacked = jnp.concatenate(
        [arrived, kicked * keep[None, :, None], jnp.zeros((6, MOVE_MAX, LANES), f32)], axis=1
    )
    moved = lax.dynamic_slice_in_dim(stacked, MOVE_MAX - before, groups + MOVE_MAX, 1)
    return jnp.transpose(moved, (1, 0, 2))


def solution(mesh):
    in_specs = (
        P(AXES, None, None),
        P(AXES, None, None),
        P(AXES, None, None),
        P(AXES, None),
        P(None, AXES),
        P(AXES),
        P(AXES, None),
        P(AXES, None, None),
        P(AXES, None, None, None),
        P(AXES, None),
        P(AXES),
    )
    return jax.shard_map(
        per_device,
        mesh=mesh,
        in_specs=in_specs,
        out_specs=P(AXES, None, None),
        check_vma=False,
    )
```

```python
import functools

import jax
import jax.numpy as jnp
from jax import lax
from jax.experimental import pallas as pl
from jax.experimental.pallas import tpu as pltpu
from jax.sharding import PartitionSpec as P

AXES = ("dom", "bulk")
MOVE_MAX = 16
SOFT_SQ = 0.001
KICK = 0.5
MID = 0.5
LANES = 128
ROWS = 32
SLOTS = 8
BATCH = 32

SMEM_SPEC = pl.BlockSpec(memory_space=pltpu.SMEM)
VMEM_SPEC = pl.BlockSpec(memory_space=pltpu.VMEM)

f32 = jnp.float32
bf16 = jnp.bfloat16


def dot(a, b):
    return lax.dot_general(a, b, (((1,), (0,)), ((), ())), preferred_element_type=f32)


def dot_t(a, b):
    return lax.dot_general(a, b, (((1,), (1,)), ((), ())), preferred_element_type=f32)


def split3(v):
    a = v.astype(bf16).astype(f32)
    r = v - a
    b = r.astype(bf16).astype(f32)
    return a, b, r - b


def split2(w):
    hi = w.astype(bf16)
    return hi, (w - hi.astype(f32)).astype(bf16)


def target_rows(x):
    rows = []
    for c in range(3):
        a, b, d = split3(x[c])
        rows += [a, a, b, b, a, d]
    rows += list(split3(x[0] * x[0] + x[1] * x[1] + x[2] * x[2]))
    one = jnp.ones_like(x[0])
    return rows + [one, one, one]


def source_rows(y, scale):
    rows = []
    for c in range(3):
        a, b, d = split3(y[c] * (-2.0 * scale))
        rows += [a, b, a, b, d, a]
    one = jnp.ones_like(y[0]) * scale
    rows += [one, one, one]
    rows += list(split3((y[0] * y[0] + y[1] * y[1] + y[2] * y[2] + SOFT_SQ) * scale))
    return rows


def inv_cube(r2):
    rs = lax.rsqrt(r2)
    return rs * rs * rs


def open_kernel(ids_ref, pos_hbm, mass_hbm, out_hbm, pos, mass, table, out, in_sem, out_sem):
    leaf_count = pos.shape[1]
    peers = out.shape[0]
    loads = [
        pltpu.make_async_copy(pos_hbm, pos, in_sem.at[0]),
        pltpu.make_async_copy(mass_hbm, mass, in_sem.at[1]),
    ]
    for load in loads:
        load.start()
    for load in loads:
        load.wait()

    def build(b, carry):
        first = pl.multiple_of(b * 8, 8)
        for c in range(4):
            v = pos[c, pl.ds(first, 8), :] if c < 3 else mass[pl.ds(first, 8), :]
            table[pl.ds(first * 8 + c, 8, stride=8), :] = v
            table[pl.ds(first * 8 + 4 + c, 8, stride=8), :] = v
        return carry

    lax.fori_loop(0, leaf_count // 8, build, 0, unroll=4)
    upper = lax.broadcasted_iota(jnp.int32, (8, LANES), 0) < 4

    def one_peer(p, carry):
        for s in range(SLOTS):
            i0 = pl.multiple_of(ids_ref[p, 2 * s] * 8, 8)
            i1 = pl.multiple_of(ids_ref[p, 2 * s + 1] * 8, 8)
            out[p, pl.ds(s * 8, 8), :] = jnp.where(
                upper, table[pl.ds(i0, 8), :], table[pl.ds(i1, 8), :]
            )
        return carry

    stores = []
    step = peers // 4
    for q in range(4):
        lax.fori_loop(q * step, (q + 1) * step, one_peer, 0, unroll=2)
        rows = pl.ds(q * step, step)
        stores.append(pltpu.make_async_copy(out.at[rows], out_hbm.at[rows], out_sem.at[q]))
        stores[-1].start()
    for store in stores:
        store.wait()


def open_leaves(ids, leaf_pos, leaf_mass):
    peers = ids.shape[0]
    shape = (peers, SLOTS * 8, LANES)
    return pl.pallas_call(
        open_kernel,
        out_shape=jax.ShapeDtypeStruct(shape, f32),
        in_specs=[
            pl.BlockSpec(memory_space=pltpu.SMEM),
            pl.BlockSpec(memory_space=pltpu.HBM),
            pl.BlockSpec(memory_space=pltpu.HBM),
        ],
        out_specs=pl.BlockSpec(memory_space=pltpu.HBM),
        scratch_shapes=[
            pltpu.VMEM(leaf_pos.shape, f32),
            pltpu.VMEM(leaf_mass.shape, f32),
            pltpu.VMEM((leaf_pos.shape[1] * 8, LANES), f32),
            pltpu.VMEM(shape, f32),
            pltpu.SemaphoreType.DMA((2,)),
            pltpu.SemaphoreType.DMA((4,)),
        ],
        compiler_params=pltpu.CompilerParams(vmem_limit_bytes=24 << 20),
        name="open_leaves",
    )(ids, leaf_pos, leaf_mass)


def local_kernel(
    eg_ref, ec_ref, pos_ref, node_ref, mass_ref, list_ref, acc_ref, todo_ref, ynt, xk, raw
):
    peers = ec_ref.shape[0]

    def enlist(p, count):
        for s in range(SLOTS):
            todo_ref[count + s] = (p * SLOTS + s) * 256 + eg_ref[s, p]
        return count + ec_ref[p]

    count = lax.fori_loop(0, peers, enlist, 0)
    for s in range(BATCH):
        todo_ref[count + s] = 0
    todo_ref[todo_ref.shape[0] - 1] = count

    nodes = node_ref.shape[1]
    y = [node_ref[c : c + 1, :] - MID for c in range(3)]
    mass = mass_ref[...]
    yk = jnp.concatenate(source_rows(y, 1.0) + [jnp.zeros((8, nodes), f32)], axis=0)
    ynt[...] = jnp.transpose(yk).astype(bf16)
    tab = jnp.concatenate([mass * y[0], mass * y[1], mass * y[2], mass], axis=0)
    tab = jnp.concatenate([tab, tab], axis=0)
    xk[...] = jnp.zeros_like(xk)
    row128 = lax.broadcasted_iota(jnp.int32, (LANES, nodes), 0)
    row16 = lax.broadcasted_iota(jnp.int32, (16, nodes), 0)
    upper = lax.broadcasted_iota(jnp.int32, (8, LANES), 0) < 4
    raw[...] = jnp.zeros_like(raw)

    def one_block(b, carry):
        first = pl.multiple_of(b * 8, 8)
        x = [pos_ref[c, pl.ds(first, 8), :] - MID for c in range(3)]
        for r, v in enumerate(target_rows(x)):
            xk[pl.ds(r, 8, stride=ROWS), :] = v
        lists = list_ref[pl.ds(first, 8), :]
        counts = []
        for g in range(8):
            wanted = lists[g : g + 1, :]
            low = jnp.where(row128 == (wanted & 127), 1.0, 0.0).astype(bf16)
            high = jnp.where(row16 == (wanted >> 7), 1.0, 0.0).astype(bf16)
            counts.append(dot_t(high, low))
        for p in range(4):
            parts = []
            for h in range(nodes // LANES):
                both = jnp.where(
                    upper, counts[2 * p][h : h + 1, :], counts[2 * p + 1][h : h + 1, :]
                )
                parts.append(tab[:, h * LANES : (h + 1) * LANES] * both)
            a, d, e = split3(jnp.concatenate(parts, axis=1))
            weights = jnp.concatenate([a, d, e, jnp.zeros_like(a)], axis=0).astype(bf16)
            xa = xk[pl.ds(2 * p * ROWS, ROWS), :]
            xb = xk[pl.ds((2 * p + 1) * ROWS, ROWS), :]
            rhs = jnp.concatenate([xa, xb], axis=1).astype(bf16)
            total = jnp.zeros((32, 2 * LANES), f32)
            for h in range(nodes // 256):
                his, los = [], []
                for k in range(256 // 128):
                    rows = pl.ds(h * 256 + k * 128, 128)
                    a, d = split2(inv_cube(dot(ynt[rows, :], rhs)))
                    his.append(a)
                    los.append(d)
                part = weights[:, h * 256 : (h + 1) * 256]
                total = total + dot(part, jnp.concatenate(his, axis=0)) + dot(part, jnp.concatenate(los, axis=0))
            total = total[0:8] + total[8:16] + total[16:24]
            raw[pl.ds(2 * p * 8, 4), :] = total[0:4, :LANES]
            raw[pl.ds((2 * p + 1) * 8, 4), :] = total[4:8, LANES:]
        weight = raw[pl.ds(3, 8, stride=8), :]
        for c in range(3):
            acc_ref[c, pl.ds(first, 8), :] = raw[pl.ds(c, 8, stride=8), :] - x[c] * weight
        return carry

    lax.fori_loop(0, acc_ref.shape[1] // 8, one_block, 0)


def local_pull(export_group, export_count, pos, node_pos, node_mass, lists):
    groups = pos.shape[1]
    nodes = node_pos.shape[1]
    entries = export_group.shape[0] * export_group.shape[1] + 2 * BATCH
    pairs = groups * LANES * nodes
    return pl.pallas_call(
        local_kernel,
        out_shape=(
            jax.ShapeDtypeStruct((3, groups, LANES), f32),
            jax.ShapeDtypeStruct((entries,), jnp.int32),
        ),
        in_specs=[SMEM_SPEC] * 2 + [VMEM_SPEC] * 4,
        out_specs=[VMEM_SPEC, SMEM_SPEC],
        scratch_shapes=[
            pltpu.VMEM((nodes, ROWS), bf16),
            pltpu.VMEM((8 * ROWS, LANES), f32),
            pltpu.VMEM((64, LANES), f32),
        ],
        compiler_params=pltpu.CompilerParams(vmem_limit_bytes=16 << 20),
        cost_estimate=pl.CostEstimate(
            flops=pairs * 2000, bytes_accessed=4 << 20, transcendentals=pairs
        ),
        name="local_pull",
    )(export_group, export_count, pos, node_pos, node_mass, lists)


def remote_kernel(
    todo, recv_ref, pos_ref, vel_ref, local_ref, out_ref, tile, place, xk, yk, tk, acc
):
    groups = pos_ref.shape[1]
    count = todo[todo.shape[0] - 1]
    xk[...] = jnp.zeros_like(xk)
    yk[...] = jnp.zeros_like(yk)
    tk[...] = jnp.zeros_like(tk)

    def clear(i, carry):
        acc[pl.ds(pl.multiple_of(i * 64, 64), 64), :] = jnp.zeros((64, LANES), f32)
        return carry

    lax.fori_loop(0, groups * 8 // 64, clear, 0)
    lane = lax.broadcasted_iota(jnp.int32, (8, LANES), 1).astype(f32)
    scale = 1.0 + lane * (1.0 / LANES)
    lift = scale * jnp.sqrt(scale)

    def one_block(b, carry):
        owners = []
        for s in range(BATCH):
            entry = todo[b * BATCH + s]
            g = entry & 255
            owners.append(g)
            tile[pl.ds(s * 8, 8), :] = recv_ref[pl.ds(pl.multiple_of((entry >> 8) * 8, 8), 8), :]
            for c in range(3):
                place[c, pl.ds(s, 1), :] = pos_ref[c, pl.ds(g, 1), :]
        for q in range(BATCH // 8):
            first = q * 8
            rank = lax.broadcasted_iota(jnp.int32, (8, LANES), 0) + (b * BATCH + first)
            x = [place[c, pl.ds(first, 8), :] - MID for c in range(3)]
            for r, v in enumerate(target_rows(x)):
                xk[pl.ds(first * ROWS + r, 8, stride=ROWS), :] = v
            for h in range(2):
                y = [tile[pl.ds(first * 8 + 4 * h + c, 8, stride=8), :] - MID for c in range(3)]
                m = tile[pl.ds(first * 8 + 4 * h + 3, 8, stride=8), :]
                m = jnp.where(rank < count, m * lift, 0.0)
                base = h * BATCH + first
                for r, v in enumerate(source_rows(y, scale)):
                    yk[pl.ds(base * ROWS + r, 8, stride=ROWS), :] = v
                for c, v in enumerate([m * y[0], m * y[1], m * y[2], m]):
                    for j, part in enumerate(split3(v)):
                        tk[pl.ds(base * 16 + 4 * j + c, 8, stride=16), :] = part
        for s in range(BATCH):
            xt = jnp.transpose(xk[pl.ds(s * ROWS, ROWS), :]).astype(bf16)
            rhs = [yk[pl.ds((h * BATCH + s) * ROWS, ROWS), :] for h in range(2)]
            r2 = dot(xt, jnp.concatenate(rhs, axis=1).astype(bf16))
            part = [tk[pl.ds((h * BATCH + s) * 16, 16), :] for h in range(2)]
            part = jnp.concatenate(part, axis=1).astype(bf16)
            total = dot_t(part, inv_cube(r2).astype(bf16))
            rows = pl.ds(pl.multiple_of(owners[s] * 8, 8), 8)
            acc[rows, :] += total[0:8] + total[8:16]
        return carry

    lax.fori_loop(0, (count + BATCH - 1) // BATCH, one_block, 0)

    def finish(b, carry):
        first = pl.multiple_of(b * 8, 8)
        rows = pl.ds(first, 8)
        total = []
        for c in range(4):
            v = acc[pl.ds(first * 8 + c, 8, stride=8), :]
            total.append(v + acc[pl.ds(first * 8 + 4 + c, 8, stride=8), :])
        for c in range(3):
            x = pos_ref[c, rows, :]
            pull = local_ref[c, rows, :] + total[c] - (x - MID) * total[3]
            out_ref[c, rows, :] = x
            out_ref[3 + c, rows, :] = vel_ref[c, rows, :] + KICK * pull
        return carry

    lax.fori_loop(0, groups // 8, finish, 0, unroll=2)


def remote_pull(todo, recv, pos, vel, local_acc):
    groups = pos.shape[1]
    return pl.pallas_call(
        remote_kernel,
        out_shape=jax.ShapeDtypeStruct((6, groups, LANES), f32),
        in_specs=[SMEM_SPEC] + [VMEM_SPEC] * 4,
        out_specs=VMEM_SPEC,
        scratch_shapes=[
            pltpu.VMEM((BATCH * 8, LANES), f32),
            pltpu.VMEM((3, BATCH, LANES), f32),
            pltpu.VMEM((BATCH * ROWS, LANES), f32),
            pltpu.VMEM((2 * BATCH * ROWS, LANES), f32),
            pltpu.VMEM((2 * BATCH * 16, LANES), f32),
            pltpu.VMEM((groups * 8, LANES), f32),
        ],
        compiler_params=pltpu.CompilerParams(vmem_limit_bytes=24 << 20),
        name="remote_pull",
    )(todo, recv, pos, vel, local_acc)


def shifted(value, axis, steps):
    count = lax.axis_size(axis)
    return lax.ppermute(value, axis, [(source, source + steps) for source in range(count - steps)])


def per_device(
    group_pos,
    group_vel,
    leaf_pos,
    leaf_mass,
    node_pos,
    node_mass,
    group_nodes,
    export_group,
    export_leaf,
    export_count,
    move_count,
):
    peers = export_group.shape[1]
    groups = group_pos.shape[0]
    asked = jnp.concatenate(
        [export_leaf[0].reshape(peers, 16), jnp.broadcast_to(move_count[:, None], (peers, 1))], axis=1
    )
    got = lax.all_to_all(asked, AXES, split_axis=0, concat_axis=0, tiled=True)
    pos = jnp.transpose(group_pos, (1, 0, 2))
    vel = jnp.transpose(group_vel, (1, 0, 2))
    mass = node_mass[None, :]
    exported = jnp.transpose(export_group[0])
    opened = open_leaves(got, jnp.transpose(leaf_pos, (1, 0, 2)), leaf_mass)
    opened, mass = lax.optimization_barrier((opened, mass))
    recv = lax.all_to_all(opened, AXES, split_axis=0, concat_axis=0, tiled=True)
    local_acc, todo = local_pull(exported, export_count[0], pos, node_pos, mass, group_nodes)
    kicked = remote_pull(todo, recv.reshape(-1, LANES), pos, vel, local_acc)
    me = lax.axis_index(AXES)
    before = jnp.where(me > 0, got[jnp.maximum(me - 1, 0), 16], 0)
    leaving = move_count[0]
    arrived = shifted(kicked[:, groups - MOVE_MAX :], AXES, 1)
    keep = (jnp.arange(groups) < groups - leaving).astype(f32)
    stacked = jnp.concatenate(
        [arrived, kicked * keep[None, :, None], jnp.zeros((6, MOVE_MAX, LANES), f32)], axis=1
    )
    moved = lax.dynamic_slice_in_dim(stacked, MOVE_MAX - before, groups + MOVE_MAX, 1)
    return jnp.transpose(moved, (1, 0, 2))


def solution(mesh):
    in_specs = (
        P(AXES, None, None),
        P(AXES, None, None),
        P(AXES, None, None),
        P(AXES, None),
        P(None, AXES),
        P(AXES),
        P(AXES, None),
        P(AXES, None, None),
        P(AXES, None, None, None),
        P(AXES, None),
        P(AXES),
    )
    return jax.shard_map(
        per_device,
        mesh=mesh,
        in_specs=in_specs,
        out_specs=P(AXES, None, None),
        check_vma=False,
    )
```

```python
import functools

import jax
import jax.numpy as jnp
from jax import lax
from jax.experimental import pallas as pl
from jax.experimental.pallas import tpu as pltpu
from jax.sharding import PartitionSpec as P

AXES = ("dom", "bulk")
MOVE_MAX = 16
SOFT_SQ = 0.001
KICK = 0.5
MID = 0.5
LANES = 128
ROWS = 32
SLOTS = 8
BATCH = 32

SMEM_SPEC = pl.BlockSpec(memory_space=pltpu.SMEM)
VMEM_SPEC = pl.BlockSpec(memory_space=pltpu.VMEM)

f32 = jnp.float32
bf16 = jnp.bfloat16


def dot(a, b):
    return lax.dot_general(a, b, (((1,), (0,)), ((), ())), preferred_element_type=f32)


def dot_t(a, b):
    return lax.dot_general(a, b, (((1,), (1,)), ((), ())), preferred_element_type=f32)


def split3(v):
    a = v.astype(bf16).astype(f32)
    r = v - a
    b = r.astype(bf16).astype(f32)
    return a, b, r - b


def split2(w):
    hi = w.astype(bf16)
    return hi, (w - hi.astype(f32)).astype(bf16)


def target_rows(x):
    rows = []
    for c in range(3):
        a, b, d = split3(x[c])
        rows += [a, a, b, b, a, d]
    rows += list(split3(x[0] * x[0] + x[1] * x[1] + x[2] * x[2]))
    one = jnp.ones_like(x[0])
    return rows + [one, one, one]


def source_rows(y, scale):
    rows = []
    for c in range(3):
        a, b, d = split3(y[c] * (-2.0 * scale))
        rows += [a, b, a, b, d, a]
    one = jnp.ones_like(y[0]) * scale
    rows += [one, one, one]
    rows += list(split3((y[0] * y[0] + y[1] * y[1] + y[2] * y[2] + SOFT_SQ) * scale))
    return rows


def inv_cube(r2):
    rs = lax.rsqrt(r2)
    return rs * rs * rs


def open_kernel(ids_ref, pos_hbm, mass_hbm, out_hbm, pos, mass, table, out, in_sem, out_sem):
    leaf_count = pos.shape[1]
    peers = out.shape[0]
    loads = []
    part = leaf_count // 1
    for q in range(1):
        rows = pl.ds(q * part, part)
        loads.append(pltpu.make_async_copy(mass_hbm.at[rows], mass.at[rows], in_sem.at[4 * q + 3]))
        for c in range(3):
            loads.append(pltpu.make_async_copy(pos_hbm.at[c, rows], pos.at[c, rows], in_sem.at[4 * q + c]))
    for load in loads:
        load.start()
    for load in loads:
        load.wait()

    def build(b, carry):
        first = pl.multiple_of(b * 8, 8)
        for c in range(4):
            v = pos[c, pl.ds(first, 8), :] if c < 3 else mass[pl.ds(first, 8), :]
            table[pl.ds(first * 8 + c, 8, stride=8), :] = v
            table[pl.ds(first * 8 + 4 + c, 8, stride=8), :] = v
        return carry

    lax.fori_loop(0, leaf_count // 8, build, 0, unroll=8)
    upper = lax.broadcasted_iota(jnp.int32, (8, LANES), 0) < 4

    def one_peer(p, carry):
        for s in range(SLOTS):
            i0 = pl.multiple_of(ids_ref[p, 2 * s] * 8, 8)
            i1 = pl.multiple_of(ids_ref[p, 2 * s + 1] * 8, 8)
            out[p, pl.ds(s * 8, 8), :] = jnp.where(
                upper, table[pl.ds(i0, 8), :], table[pl.ds(i1, 8), :]
            )
        return carry

    stores = []
    step = peers // 32
    for q in range(32):
        lax.fori_loop(q * step, (q + 1) * step, one_peer, 0, unroll=4)
        rows = pl.ds(q * step, step)
        stores.append(pltpu.make_async_copy(out.at[rows], out_hbm.at[rows], out_sem.at[q]))
        stores[-1].start()
    for store in stores:
        store.wait()


def open_leaves(ids, leaf_pos, leaf_mass):
    peers = ids.shape[0]
    shape = (peers, SLOTS * 8, LANES)
    return pl.pallas_call(
        open_kernel,
        out_shape=jax.ShapeDtypeStruct(shape, f32),
        in_specs=[
            pl.BlockSpec(memory_space=pltpu.SMEM),
            pl.BlockSpec(memory_space=pltpu.HBM),
            pl.BlockSpec(memory_space=pltpu.HBM),
        ],
        out_specs=pl.BlockSpec(memory_space=pltpu.HBM),
        scratch_shapes=[
            pltpu.VMEM(leaf_pos.shape, f32),
            pltpu.VMEM(leaf_mass.shape, f32),
            pltpu.VMEM((leaf_pos.shape[1] * 8, LANES), f32),
            pltpu.VMEM(shape, f32),
            pltpu.SemaphoreType.DMA((4,)),
            pltpu.SemaphoreType.DMA((32,)),
        ],
        compiler_params=pltpu.CompilerParams(vmem_limit_bytes=60 << 20),
        name="open_leaves",
    )(ids, leaf_pos, leaf_mass)


def local_kernel(
    eg_ref, ec_ref, pos_ref, node_ref, mass_ref, list_ref, acc_ref, todo_ref, ynt, xk, raw
):
    peers = ec_ref.shape[0]

    def enlist(p, count):
        for s in range(SLOTS):
            todo_ref[count + s] = (p * SLOTS + s) * 256 + eg_ref[s, p]
        return count + ec_ref[p]

    count = lax.fori_loop(0, peers, enlist, 0)
    for s in range(BATCH):
        todo_ref[count + s] = 0
    todo_ref[todo_ref.shape[0] - 1] = count

    nodes = node_ref.shape[1]
    y = [node_ref[c : c + 1, :] - MID for c in range(3)]
    mass = mass_ref[...]
    yk = jnp.concatenate(source_rows(y, 1.0) + [jnp.zeros((8, nodes), f32)], axis=0)
    ynt[...] = jnp.transpose(yk).astype(bf16)
    tab = jnp.concatenate([mass * y[0], mass * y[1], mass * y[2], mass], axis=0)
    tab = jnp.concatenate([tab, tab], axis=0)
    xk[...] = jnp.zeros_like(xk)
    row128 = lax.broadcasted_iota(jnp.int32, (LANES, nodes), 0)
    row16 = lax.broadcasted_iota(jnp.int32, (16, nodes), 0)
    upper = lax.broadcasted_iota(jnp.int32, (8, LANES), 0) < 4
    raw[...] = jnp.zeros_like(raw)

    def one_block(b, carry):
        first = pl.multiple_of(b * 8, 8)
        x = [pos_ref[c, pl.ds(first, 8), :] - MID for c in range(3)]
        for r, v in enumerate(target_rows(x)):
            xk[pl.ds(r, 8, stride=ROWS), :] = v
        lists = list_ref[pl.ds(first, 8), :]
        counts = []
        for g in range(8):
            wanted = lists[g : g + 1, :]
            low = jnp.where(row128 == (wanted & 127), 1.0, 0.0).astype(bf16)
            high = jnp.where(row16 == (wanted >> 7), 1.0, 0.0).astype(bf16)
            counts.append(dot_t(high, low))
        for p in range(4):
            parts = []
            for h in range(nodes // LANES):
                both = jnp.where(
                    upper, counts[2 * p][h : h + 1, :], counts[2 * p + 1][h : h + 1, :]
                )
                parts.append(tab[:, h * LANES : (h + 1) * LANES] * both)
            a, d, e = split3(jnp.concatenate(parts, axis=1))
            weights = jnp.concatenate([a, d, e, jnp.zeros_like(a)], axis=0).astype(bf16)
            xa = xk[pl.ds(2 * p * ROWS, ROWS), :]
            xb = xk[pl.ds((2 * p + 1) * ROWS, ROWS), :]
            rhs = jnp.concatenate([xa, xb], axis=1).astype(bf16)
            total = jnp.zeros((32, 2 * LANES), f32)
            for h in range(nodes // 256):
                his, los = [], []
                for k in range(256 // 128):
                    rows = pl.ds(h * 256 + k * 128, 128)
                    a, d = split2(inv_cube(dot(ynt[rows, :], rhs)))
                    his.append(a)
                    los.append(d)
                part = weights[:, h * 256 : (h + 1) * 256]
                total = total + dot(part, jnp.concatenate(his, axis=0)) + dot(part, jnp.concatenate(los, axis=0))
            total = total[0:8] + total[8:16] + total[16:24]
            raw[pl.ds(2 * p * 8, 4), :] = total[0:4, :LANES]
            raw[pl.ds((2 * p + 1) * 8, 4), :] = total[4:8, LANES:]
        weight = raw[pl.ds(3, 8, stride=8), :]
        for c in range(3):
            acc_ref[c, pl.ds(first, 8), :] = raw[pl.ds(c, 8, stride=8), :] - x[c] * weight
        return carry

    lax.fori_loop(0, acc_ref.shape[1] // 8, one_block, 0)


def local_pull(export_group, export_count, pos, node_pos, node_mass, lists):
    groups = pos.shape[1]
    nodes = node_pos.shape[1]
    entries = export_group.shape[0] * export_group.shape[1] + 2 * BATCH
    pairs = groups * LANES * nodes
    return pl.pallas_call(
        local_kernel,
        out_shape=(
            jax.ShapeDtypeStruct((3, groups, LANES), f32),
            jax.ShapeDtypeStruct((entries,), jnp.int32),
        ),
        in_specs=[SMEM_SPEC] * 2 + [VMEM_SPEC] * 4,
        out_specs=[VMEM_SPEC, SMEM_SPEC],
        scratch_shapes=[
            pltpu.VMEM((nodes, ROWS), bf16),
            pltpu.VMEM((8 * ROWS, LANES), f32),
            pltpu.VMEM((64, LANES), f32),
        ],
        compiler_params=pltpu.CompilerParams(vmem_limit_bytes=16 << 20),
        cost_estimate=pl.CostEstimate(
            flops=pairs * 2000, bytes_accessed=4 << 20, transcendentals=pairs
        ),
        name="local_pull",
    )(export_group, export_count, pos, node_pos, node_mass, lists)


def remote_kernel(
    todo, recv_ref, pos_ref, vel_ref, local_ref, out_ref, tile, place, xk, yk, tk, acc
):
    groups = pos_ref.shape[1]
    count = todo[todo.shape[0] - 1]
    xk[...] = jnp.zeros_like(xk)
    yk[...] = jnp.zeros_like(yk)
    tk[...] = jnp.zeros_like(tk)

    def clear(i, carry):
        acc[pl.ds(pl.multiple_of(i * 64, 64), 64), :] = jnp.zeros((64, LANES), f32)
        return carry

    lax.fori_loop(0, groups * 8 // 64, clear, 0)
    lane = lax.broadcasted_iota(jnp.int32, (8, LANES), 1).astype(f32)
    scale = 1.0 + lane * (1.0 / LANES)
    lift = scale * jnp.sqrt(scale)

    def one_block(b, carry):
        owners = []
        for s in range(BATCH):
            entry = todo[b * BATCH + s]
            g = entry & 255
            owners.append(g)
            tile[pl.ds(s * 8, 8), :] = recv_ref[pl.ds(pl.multiple_of((entry >> 8) * 8, 8), 8), :]
            for c in range(3):
                place[c, pl.ds(s, 1), :] = pos_ref[c, pl.ds(g, 1), :]
        for q in range(BATCH // 8):
            first = q * 8
            rank = lax.broadcasted_iota(jnp.int32, (8, LANES), 0) + (b * BATCH + first)
            x = [place[c, pl.ds(first, 8), :] - MID for c in range(3)]
            for r, v in enumerate(target_rows(x)):
                xk[pl.ds(first * ROWS + r, 8, stride=ROWS), :] = v
            for h in range(2):
                y = [tile[pl.ds(first * 8 + 4 * h + c, 8, stride=8), :] - MID for c in range(3)]
                m = tile[pl.ds(first * 8 + 4 * h + 3, 8, stride=8), :]
                m = jnp.where(rank < count, m * lift, 0.0)
                base = h * BATCH + first
                for r, v in enumerate(source_rows(y, scale)):
                    yk[pl.ds(base * ROWS + r, 8, stride=ROWS), :] = v
                for c, v in enumerate([m * y[0], m * y[1], m * y[2], m]):
                    for j, part in enumerate(split3(v)):
                        tk[pl.ds(base * 16 + 4 * j + c, 8, stride=16), :] = part
        for s in range(BATCH):
            xt = jnp.transpose(xk[pl.ds(s * ROWS, ROWS), :]).astype(bf16)
            rhs = [yk[pl.ds((h * BATCH + s) * ROWS, ROWS), :] for h in range(2)]
            r2 = dot(xt, jnp.concatenate(rhs, axis=1).astype(bf16))
            part = [tk[pl.ds((h * BATCH + s) * 16, 16), :] for h in range(2)]
            part = jnp.concatenate(part, axis=1).astype(bf16)
            total = dot_t(part, inv_cube(r2).astype(bf16))
            rows = pl.ds(pl.multiple_of(owners[s] * 8, 8), 8)
            acc[rows, :] += total[0:8] + total[8:16]
        return carry

    lax.fori_loop(0, (count + BATCH - 1) // BATCH, one_block, 0)

    def finish(b, carry):
        first = pl.multiple_of(b * 8, 8)
        rows = pl.ds(first, 8)
        total = []
        for c in range(4):
            v = acc[pl.ds(first * 8 + c, 8, stride=8), :]
            total.append(v + acc[pl.ds(first * 8 + 4 + c, 8, stride=8), :])
        for c in range(3):
            x = pos_ref[c, rows, :]
            pull = local_ref[c, rows, :] + total[c] - (x - MID) * total[3]
            out_ref[c, rows, :] = x
            out_ref[3 + c, rows, :] = vel_ref[c, rows, :] + KICK * pull
        return carry

    lax.fori_loop(0, groups // 8, finish, 0, unroll=2)


def remote_pull(todo, recv, pos, vel, local_acc):
    groups = pos.shape[1]
    return pl.pallas_call(
        remote_kernel,
        out_shape=jax.ShapeDtypeStruct((6, groups, LANES), f32),
        in_specs=[SMEM_SPEC] + [VMEM_SPEC] * 4,
        out_specs=VMEM_SPEC,
        scratch_shapes=[
            pltpu.VMEM((BATCH * 8, LANES), f32),
            pltpu.VMEM((3, BATCH, LANES), f32),
            pltpu.VMEM((BATCH * ROWS, LANES), f32),
            pltpu.VMEM((2 * BATCH * ROWS, LANES), f32),
            pltpu.VMEM((2 * BATCH * 16, LANES), f32),
            pltpu.VMEM((groups * 8, LANES), f32),
        ],
        compiler_params=pltpu.CompilerParams(vmem_limit_bytes=24 << 20),
        name="remote_pull",
    )(todo, recv, pos, vel, local_acc)


def shifted(value, axis, steps):
    count = lax.axis_size(axis)
    return lax.ppermute(value, axis, [(source, source + steps) for source in range(count - steps)])


def per_device(
    group_pos,
    group_vel,
    leaf_pos,
    leaf_mass,
    node_pos,
    node_mass,
    group_nodes,
    export_group,
    export_leaf,
    export_count,
    move_count,
):
    peers = export_group.shape[1]
    groups = group_pos.shape[0]
    asked = jnp.concatenate(
        [export_leaf[0].reshape(peers, 16), jnp.broadcast_to(move_count[:, None], (peers, 1))], axis=1
    )
    got = lax.all_to_all(asked, AXES, split_axis=0, concat_axis=0, tiled=True)
    pos = jnp.transpose(group_pos, (1, 0, 2))
    vel = jnp.transpose(group_vel, (1, 0, 2))
    mass = node_mass[None, :]
    exported = jnp.transpose(export_group[0])
    opened = open_leaves(got, jnp.transpose(leaf_pos, (1, 0, 2)), leaf_mass)
    opened, mass = lax.optimization_barrier((opened, mass))
    recv = lax.all_to_all(opened, AXES, split_axis=0, concat_axis=0, tiled=True)
    local_acc, todo = local_pull(exported, export_count[0], pos, node_pos, mass, group_nodes)
    kicked = remote_pull(todo, recv.reshape(-1, LANES), pos, vel, local_acc)
    me = lax.axis_index(AXES)
    before = jnp.where(me > 0, got[jnp.maximum(me - 1, 0), 16], 0)
    leaving = move_count[0]
    arrived = shifted(kicked[:, groups - MOVE_MAX :], AXES, 1)
    keep = (jnp.arange(groups) < groups - leaving).astype(f32)
    stacked = jnp.concatenate(
        [arrived, kicked * keep[None, :, None], jnp.zeros((6, MOVE_MAX, LANES), f32)], axis=1
    )
    moved = lax.dynamic_slice_in_dim(stacked, MOVE_MAX - before, groups + MOVE_MAX, 1)
    return jnp.transpose(moved, (1, 0, 2))


def solution(mesh):
    in_specs = (
        P(AXES, None, None),
        P(AXES, None, None),
        P(AXES, None, None),
        P(AXES, None),
        P(None, AXES),
        P(AXES),
        P(AXES, None),
        P(AXES, None, None),
        P(AXES, None, None, None),
        P(AXES, None),
        P(AXES),
    )
    return jax.shard_map(
        per_device,
        mesh=mesh,
        in_specs=in_specs,
        out_specs=P(AXES, None, None),
        check_vma=False,
    )
```

```python
import functools

import jax
import jax.numpy as jnp
from jax import lax
from jax.experimental import pallas as pl
from jax.experimental.pallas import tpu as pltpu
from jax.sharding import PartitionSpec as P

AXES = ("dom", "bulk")
MOVE_MAX = 16
SOFT_SQ = 0.001
KICK = 0.5
MID = 0.5
LANES = 128
ROWS = 32
SLOTS = 8
TOGETHER = 32
BATCH = 64
TAIL = 16

SMEM_SPEC = pl.BlockSpec(memory_space=pltpu.SMEM)
VMEM_SPEC = pl.BlockSpec(memory_space=pltpu.VMEM)

f32 = jnp.float32
bf16 = jnp.bfloat16


def dot(a, b):
    return lax.dot_general(a, b, (((1,), (0,)), ((), ())), preferred_element_type=f32)


def dot_t(a, b):
    return lax.dot_general(a, b, (((1,), (1,)), ((), ())), preferred_element_type=f32)


def split3(v):
    a = v.astype(bf16).astype(f32)
    r = v - a
    b = r.astype(bf16).astype(f32)
    return a, b, r - b


def split2(w):
    hi = w.astype(bf16)
    return hi, (w - hi.astype(f32)).astype(bf16)


def target_rows(x):
    rows = []
    for c in range(3):
        a, b, d = split3(x[c])
        rows += [a, a, b, b, a, d]
    rows += list(split3(x[0] * x[0] + x[1] * x[1] + x[2] * x[2]))
    one = jnp.ones_like(x[0])
    return rows + [one, one, one]


def source_rows(y, scale):
    rows = []
    for c in range(3):
        a, b, d = split3(y[c] * (-2.0 * scale))
        rows += [a, b, a, b, d, a]
    one = jnp.ones_like(y[0]) * scale
    rows += [one, one, one]
    rows += list(split3((y[0] * y[0] + y[1] * y[1] + y[2] * y[2] + SOFT_SQ) * scale))
    return rows


def inv_cube(r2):
    rs = lax.rsqrt(r2)
    return rs * rs * rs


def open_kernel(ids_ref, pos_hbm, mass_hbm, out_hbm, pos, mass, table, out, in_sem, out_sem):
    leaf_count = pos.shape[1]
    peers = out.shape[0]
    loads = []
    part = leaf_count // 1
    for q in range(1):
        rows = pl.ds(q * part, part)
        loads.append(pltpu.make_async_copy(mass_hbm.at[rows], mass.at[rows], in_sem.at[4 * q + 3]))
        for c in range(3):
            loads.append(pltpu.make_async_copy(pos_hbm.at[c, rows], pos.at[c, rows], in_sem.at[4 * q + c]))
    for load in loads:
        load.start()
    for load in loads:
        load.wait()

    def build(b, carry):
        first = pl.multiple_of(b * 8, 8)
        for c in range(4):
            v = pos[c, pl.ds(first, 8), :] if c < 3 else mass[pl.ds(first, 8), :]
            table[pl.ds(first * 8 + c, 8, stride=8), :] = v
            table[pl.ds(first * 8 + 4 + c, 8, stride=8), :] = v
        return carry

    lax.fori_loop(0, leaf_count // 8, build, 0, unroll=8)
    upper = lax.broadcasted_iota(jnp.int32, (8, LANES), 0) < 4

    def one_peer(p, carry):
        for s in range(SLOTS):
            i0 = pl.multiple_of(ids_ref[p, 2 * s] * 8, 8)
            i1 = pl.multiple_of(ids_ref[p, 2 * s + 1] * 8, 8)
            out[p, pl.ds(s * 8, 8), :] = jnp.where(
                upper, table[pl.ds(i0, 8), :], table[pl.ds(i1, 8), :]
            )
        return carry

    stores = []
    step = peers // 32
    for q in range(32):
        lax.fori_loop(q * step, (q + 1) * step, one_peer, 0, unroll=4)
        rows = pl.ds(q * step, step)
        stores.append(pltpu.make_async_copy(out.at[rows], out_hbm.at[rows], out_sem.at[q]))
        stores[-1].start()
    for store in stores:
        store.wait()


def open_leaves(ids, leaf_pos, leaf_mass):
    peers = ids.shape[0]
    shape = (peers, SLOTS * 8, LANES)
    return pl.pallas_call(
        open_kernel,
        out_shape=jax.ShapeDtypeStruct(shape, f32),
        in_specs=[
            pl.BlockSpec(memory_space=pltpu.SMEM),
            pl.BlockSpec(memory_space=pltpu.HBM),
            pl.BlockSpec(memory_space=pltpu.HBM),
        ],
        out_specs=pl.BlockSpec(memory_space=pltpu.HBM),
        scratch_shapes=[
            pltpu.VMEM(leaf_pos.shape, f32),
            pltpu.VMEM(leaf_mass.shape, f32),
            pltpu.VMEM((leaf_pos.shape[1] * 8, LANES), f32),
            pltpu.VMEM(shape, f32),
            pltpu.SemaphoreType.DMA((4,)),
            pltpu.SemaphoreType.DMA((32,)),
        ],
        compiler_params=pltpu.CompilerParams(vmem_limit_bytes=60 << 20),
        name="open_leaves",
    )(ids, leaf_pos, leaf_mass)


def local_kernel(
    eg_ref, ec_ref, pos_ref, node_ref, mass_ref, list_ref, acc_ref, todo_ref, ynt, xk, raw
):
    peers = ec_ref.shape[0]

    def enlist(p, count):
        for s in range(SLOTS):
            todo_ref[count + s] = (p * SLOTS + s) * 256 + eg_ref[s, p]
        return count + ec_ref[p]

    count = lax.fori_loop(0, peers, enlist, 0)
    for s in range(BATCH):
        todo_ref[count + s] = 0
    todo_ref[todo_ref.shape[0] - 1] = count

    nodes = node_ref.shape[1]
    y = [node_ref[c : c + 1, :] - MID for c in range(3)]
    mass = mass_ref[...]
    yk = jnp.concatenate(source_rows(y, 1.0) + [jnp.zeros((8, nodes), f32)], axis=0)
    ynt[...] = jnp.transpose(yk).astype(bf16)
    tab = jnp.concatenate([mass * y[0], mass * y[1], mass * y[2], mass], axis=0)
    tab = jnp.concatenate([tab, tab], axis=0)
    xk[...] = jnp.zeros_like(xk)
    row128 = lax.broadcasted_iota(jnp.int32, (LANES, nodes), 0)
    row16 = lax.broadcasted_iota(jnp.int32, (16, nodes), 0)
    upper = lax.broadcasted_iota(jnp.int32, (8, LANES), 0) < 4
    raw[...] = jnp.zeros_like(raw)

    def one_block(b, carry):
        first = pl.multiple_of(b * TOGETHER, TOGETHER)
        places = []
        for q in range(TOGETHER // 8):
            x = [pos_ref[c, pl.ds(first + q * 8, 8), :] - MID for c in range(3)]
            places.append(x)
            for r, v in enumerate(target_rows(x)):
                xk[pl.ds(q * 8 * ROWS + r, 8, stride=ROWS), :] = v
        lists = list_ref[pl.ds(first, TOGETHER), :]
        counts = []
        for g in range(TOGETHER):
            wanted = lists[g : g + 1, :]
            low = jnp.where(row128 == (wanted & 127), 1.0, 0.0).astype(bf16)
            high = jnp.where(row16 == (wanted >> 7), 1.0, 0.0).astype(bf16)
            counts.append(dot_t(high, low))
        for p in range(TOGETHER // 2):
            parts = []
            for h in range(nodes // LANES):
                both = jnp.where(
                    upper, counts[2 * p][h : h + 1, :], counts[2 * p + 1][h : h + 1, :]
                )
                parts.append(tab[:, h * LANES : (h + 1) * LANES] * both)
            a, d, e = split3(jnp.concatenate(parts, axis=1))
            weights = jnp.concatenate([a, d, e, jnp.zeros_like(a)], axis=0).astype(bf16)
            xa = xk[pl.ds(2 * p * ROWS, ROWS), :]
            xb = xk[pl.ds((2 * p + 1) * ROWS, ROWS), :]
            rhs = jnp.concatenate([xa, xb], axis=1).astype(bf16)
            total = jnp.zeros((32, 2 * LANES), f32)
            for h in range(nodes // 256):
                his, los = [], []
                for k in range(256 // 128):
                    rows = pl.ds(h * 256 + k * 128, 128)
                    a, d = split2(inv_cube(dot(ynt[rows, :], rhs)))
                    his.append(a)
                    los.append(d)
                part = weights[:, h * 256 : (h + 1) * 256]
                total = total + dot(part, jnp.concatenate(his, axis=0)) + dot(part, jnp.concatenate(los, axis=0))
            total = total[0:8] + total[8:16] + total[16:24]
            raw[pl.ds(2 * p * 8, 4), :] = total[0:4, :LANES]
            raw[pl.ds((2 * p + 1) * 8, 4), :] = total[4:8, LANES:]
        for q, x in enumerate(places):
            weight = raw[pl.ds(q * 64 + 3, 8, stride=8), :]
            for c in range(3):
                pull = raw[pl.ds(q * 64 + c, 8, stride=8), :] - x[c] * weight
                acc_ref[c, pl.ds(first + q * 8, 8), :] = pull
        return carry

    lax.fori_loop(0, acc_ref.shape[1] // TOGETHER, one_block, 0)


def local_pull(export_group, export_count, pos, node_pos, node_mass, lists):
    groups = pos.shape[1]
    nodes = node_pos.shape[1]
    entries = export_group.shape[0] * export_group.shape[1] + 2 * BATCH
    pairs = groups * LANES * nodes
    return pl.pallas_call(
        local_kernel,
        out_shape=(
            jax.ShapeDtypeStruct((3, groups, LANES), f32),
            jax.ShapeDtypeStruct((entries,), jnp.int32),
        ),
        in_specs=[SMEM_SPEC] * 2 + [VMEM_SPEC] * 4,
        out_specs=[VMEM_SPEC, SMEM_SPEC],
        scratch_shapes=[
            pltpu.VMEM((nodes, ROWS), bf16),
            pltpu.VMEM((TOGETHER * ROWS, LANES), f32),
            pltpu.VMEM((TOGETHER * 8, LANES), f32),
        ],
        compiler_params=pltpu.CompilerParams(vmem_limit_bytes=16 << 20),
        cost_estimate=pl.CostEstimate(
            flops=pairs * 2000, bytes_accessed=4 << 20, transcendentals=pairs
        ),
        name="local_pull",
    )(export_group, export_count, pos, node_pos, node_mass, lists)


def remote_kernel(
    todo, recv_ref, pos_ref, vel_ref, local_ref, out_ref, tile, place, xk, yk, tk, acc
):
    groups = pos_ref.shape[1]
    count = todo[todo.shape[0] - 1]
    xk[...] = jnp.zeros_like(xk)
    yk[...] = jnp.zeros_like(yk)
    tk[...] = jnp.zeros_like(tk)

    def clear(i, carry):
        acc[pl.ds(pl.multiple_of(i * 64, 64), 64), :] = jnp.zeros((64, LANES), f32)
        return carry

    lax.fori_loop(0, groups * 8 // 64, clear, 0)
    lane = lax.broadcasted_iota(jnp.int32, (8, LANES), 1).astype(f32)
    scale = 1.0 + lane * (1.0 / LANES)
    lift = scale * jnp.sqrt(scale)

    def one_batch(size, start, b, carry):
        owners = []
        for s in range(size):
            entry = todo[start + b * size + s]
            g = entry & 255
            owners.append(g)
            tile[pl.ds(s * 8, 8), :] = recv_ref[pl.ds(pl.multiple_of((entry >> 8) * 8, 8), 8), :]
            for c in range(3):
                place[c, pl.ds(s, 1), :] = pos_ref[c, pl.ds(g, 1), :]
        for q in range(size // 8):
            first = q * 8
            rank = lax.broadcasted_iota(jnp.int32, (8, LANES), 0) + (start + b * size + first)
            x = [place[c, pl.ds(first, 8), :] - MID for c in range(3)]
            for r, v in enumerate(target_rows(x)):
                xk[pl.ds(first * ROWS + r, 8, stride=ROWS), :] = v
            for h in range(2):
                y = [tile[pl.ds(first * 8 + 4 * h + c, 8, stride=8), :] - MID for c in range(3)]
                m = tile[pl.ds(first * 8 + 4 * h + 3, 8, stride=8), :]
                m = jnp.where(rank < count, m * lift, 0.0)
                base = h * BATCH + first
                for r, v in enumerate(source_rows(y, scale)):
                    yk[pl.ds(base * ROWS + r, 8, stride=ROWS), :] = v
                for c, v in enumerate([m * y[0], m * y[1], m * y[2], m]):
                    for j, part in enumerate(split3(v)):
                        tk[pl.ds(base * 16 + 4 * j + c, 8, stride=16), :] = part
        for s in range(size):
            xt = jnp.transpose(xk[pl.ds(s * ROWS, ROWS), :]).astype(bf16)
            rhs = [yk[pl.ds((h * BATCH + s) * ROWS, ROWS), :] for h in range(2)]
            r2 = dot(xt, jnp.concatenate(rhs, axis=1).astype(bf16))
            part = [tk[pl.ds((h * BATCH + s) * 16, 16), :] for h in range(2)]
            part = jnp.concatenate(part, axis=1).astype(bf16)
            total = dot_t(part, inv_cube(r2).astype(bf16))
            rows = pl.ds(pl.multiple_of(owners[s] * 8, 8), 8)
            acc[rows, :] += total[0:8] + total[8:16]
        return carry

    whole = count // BATCH
    lax.fori_loop(0, whole, functools.partial(one_batch, BATCH, 0), 0)
    rest = count - whole * BATCH
    lax.fori_loop(0, (rest + TAIL - 1) // TAIL, functools.partial(one_batch, TAIL, whole * BATCH), 0)

    def finish(b, carry):
        first = pl.multiple_of(b * 8, 8)
        rows = pl.ds(first, 8)
        total = []
        for c in range(4):
            v = acc[pl.ds(first * 8 + c, 8, stride=8), :]
            total.append(v + acc[pl.ds(first * 8 + 4 + c, 8, stride=8), :])
        for c in range(3):
            x = pos_ref[c, rows, :]
            pull = local_ref[c, rows, :] + total[c] - (x - MID) * total[3]
            out_ref[c, rows, :] = x
            out_ref[3 + c, rows, :] = vel_ref[c, rows, :] + KICK * pull
        return carry

    lax.fori_loop(0, groups // 8, finish, 0, unroll=2)


def remote_pull(todo, recv, pos, vel, local_acc):
    groups = pos.shape[1]
    return pl.pallas_call(
        remote_kernel,
        out_shape=jax.ShapeDtypeStruct((6, groups, LANES), f32),
        in_specs=[SMEM_SPEC] + [VMEM_SPEC] * 4,
        out_specs=VMEM_SPEC,
        scratch_shapes=[
            pltpu.VMEM((BATCH * 8, LANES), f32),
            pltpu.VMEM((3, BATCH, LANES), f32),
            pltpu.VMEM((BATCH * ROWS, LANES), f32),
            pltpu.VMEM((2 * BATCH * ROWS, LANES), f32),
            pltpu.VMEM((2 * BATCH * 16, LANES), f32),
            pltpu.VMEM((groups * 8, LANES), f32),
        ],
        compiler_params=pltpu.CompilerParams(vmem_limit_bytes=24 << 20),
        name="remote_pull",
    )(todo, recv, pos, vel, local_acc)


def shifted(value, axis, steps):
    count = lax.axis_size(axis)
    return lax.ppermute(value, axis, [(source, source + steps) for source in range(count - steps)])


def per_device(
    group_pos,
    group_vel,
    leaf_pos,
    leaf_mass,
    node_pos,
    node_mass,
    group_nodes,
    export_group,
    export_leaf,
    export_count,
    move_count,
):
    peers = export_group.shape[1]
    groups = group_pos.shape[0]
    asked = jnp.concatenate(
        [export_leaf[0].reshape(peers, 16), jnp.broadcast_to(move_count[:, None], (peers, 1))], axis=1
    )
    got = lax.all_to_all(asked, AXES, split_axis=0, concat_axis=0, tiled=True)
    pos = jnp.transpose(group_pos, (1, 0, 2))
    vel = jnp.transpose(group_vel, (1, 0, 2))
    mass = node_mass[None, :]
    exported = jnp.transpose(export_group[0])
    opened = open_leaves(got, jnp.transpose(leaf_pos, (1, 0, 2)), leaf_mass)
    opened, mass = lax.optimization_barrier((opened, mass))
    recv = lax.all_to_all(opened, AXES, split_axis=0, concat_axis=0, tiled=True)
    local_acc, todo = local_pull(exported, export_count[0], pos, node_pos, mass, group_nodes)
    kicked = remote_pull(todo, recv.reshape(-1, LANES), pos, vel, local_acc)
    me = lax.axis_index(AXES)
    before = jnp.where(me > 0, got[jnp.maximum(me - 1, 0), 16], 0)
    leaving = move_count[0]
    arrived = shifted(kicked[:, groups - MOVE_MAX :], AXES, 1)
    keep = (jnp.arange(groups) < groups - leaving).astype(f32)
    stacked = jnp.concatenate(
        [arrived, kicked * keep[None, :, None], jnp.zeros((6, MOVE_MAX, LANES), f32)], axis=1
    )
    moved = lax.dynamic_slice_in_dim(stacked, MOVE_MAX - before, groups + MOVE_MAX, 1)
    return jnp.transpose(moved, (1, 0, 2))


def solution(mesh):
    in_specs = (
        P(AXES, None, None),
        P(AXES, None, None),
        P(AXES, None, None),
        P(AXES, None),
        P(None, AXES),
        P(AXES),
        P(AXES, None),
        P(AXES, None, None),
        P(AXES, None, None, None),
        P(AXES, None),
        P(AXES),
    )
    return jax.shard_map(
        per_device,
        mesh=mesh,
        in_specs=in_specs,
        out_specs=P(AXES, None, None),
        check_vma=False,
    )
```

```python
import functools

import jax
import jax.numpy as jnp
from jax import lax
from jax.experimental import pallas as pl
from jax.experimental.pallas import tpu as pltpu
from jax.sharding import PartitionSpec as P

AXES = ("dom", "bulk")
MOVE_MAX = 16
SOFT_SQ = 0.001
KICK = 0.5
MID = 0.5
LANES = 128
ROWS = 32
SLOTS = 8
TOGETHER = 32
BATCH = 64
TAIL = 16

SMEM_SPEC = pl.BlockSpec(memory_space=pltpu.SMEM)
VMEM_SPEC = pl.BlockSpec(memory_space=pltpu.VMEM)

f32 = jnp.float32
bf16 = jnp.bfloat16


def dot(a, b):
    return lax.dot_general(a, b, (((1,), (0,)), ((), ())), preferred_element_type=f32)


def dot_t(a, b):
    return lax.dot_general(a, b, (((1,), (1,)), ((), ())), preferred_element_type=f32)


def split3(v):
    a = v.astype(bf16).astype(f32)
    r = v - a
    b = r.astype(bf16).astype(f32)
    return a, b, r - b


def split2(w):
    hi = w.astype(bf16)
    return hi, (w - hi.astype(f32)).astype(bf16)


def target_rows(x):
    rows = []
    for c in range(3):
        a, b, d = split3(x[c])
        rows += [a, a, b, b, a, d]
    rows += list(split3(x[0] * x[0] + x[1] * x[1] + x[2] * x[2]))
    one = jnp.ones_like(x[0])
    return rows + [one, one, one]


def source_rows(y, scale):
    rows = []
    for c in range(3):
        a, b, d = split3(y[c] * (-2.0 * scale))
        rows += [a, b, a, b, d, a]
    one = jnp.ones_like(y[0]) * scale
    rows += [one, one, one]
    rows += list(split3((y[0] * y[0] + y[1] * y[1] + y[2] * y[2] + SOFT_SQ) * scale))
    return rows


def inv_cube(r2):
    rs = lax.rsqrt(r2)
    return rs * rs * rs


def open_kernel(
    ids_any, pos_hbm, mass_hbm, out_hbm, ids_ref, pos, mass, table, out, ids_sem, in_sem, out_sem
):
    fetch = pltpu.make_async_copy(ids_any, ids_ref, ids_sem)
    fetch.start()
    leaf_count = pos.shape[1]
    peers = out.shape[0]
    loads = []
    part = leaf_count // 1
    for q in range(1):
        rows = pl.ds(q * part, part)
        loads.append(pltpu.make_async_copy(mass_hbm.at[rows], mass.at[rows], in_sem.at[4 * q + 3]))
        for c in range(3):
            loads.append(pltpu.make_async_copy(pos_hbm.at[c, rows], pos.at[c, rows], in_sem.at[4 * q + c]))
    for load in loads:
        load.start()
    for load in loads:
        load.wait()

    def build(b, carry):
        first = pl.multiple_of(b * 8, 8)
        for c in range(4):
            v = pos[c, pl.ds(first, 8), :] if c < 3 else mass[pl.ds(first, 8), :]
            table[pl.ds(first * 8 + c, 8, stride=8), :] = v
            table[pl.ds(first * 8 + 4 + c, 8, stride=8), :] = v
        return carry

    lax.fori_loop(0, leaf_count // 8, build, 0, unroll=8)
    upper = lax.broadcasted_iota(jnp.int32, (8, LANES), 0) < 4

    def one_peer(p, carry):
        for s in range(SLOTS):
            i0 = pl.multiple_of(ids_ref[p, 2 * s] * 8, 8)
            i1 = pl.multiple_of(ids_ref[p, 2 * s + 1] * 8, 8)
            out[p, pl.ds(s * 8, 8), :] = jnp.where(
                upper, table[pl.ds(i0, 8), :], table[pl.ds(i1, 8), :]
            )
        return carry

    fetch.wait()
    stores = []
    step = peers // 32
    for q in range(32):
        lax.fori_loop(q * step, (q + 1) * step, one_peer, 0, unroll=4)
        rows = pl.ds(q * step, step)
        stores.append(pltpu.make_async_copy(out.at[rows], out_hbm.at[rows], out_sem.at[q]))
        stores[-1].start()
    for store in stores:
        store.wait()


def open_leaves(ids, leaf_pos, leaf_mass):
    peers = ids.shape[0]
    shape = (peers, SLOTS * 8, LANES)
    return pl.pallas_call(
        open_kernel,
        out_shape=jax.ShapeDtypeStruct(shape, f32),
        in_specs=[
            pl.BlockSpec(memory_space=pl.ANY),
            pl.BlockSpec(memory_space=pltpu.HBM),
            pl.BlockSpec(memory_space=pltpu.HBM),
        ],
        out_specs=pl.BlockSpec(memory_space=pltpu.HBM),
        scratch_shapes=[
            pltpu.SMEM(ids.shape, jnp.int32),
            pltpu.VMEM(leaf_pos.shape, f32),
            pltpu.VMEM(leaf_mass.shape, f32),
            pltpu.VMEM((leaf_pos.shape[1] * 8, LANES), f32),
            pltpu.VMEM(shape, f32),
            pltpu.SemaphoreType.DMA,
            pltpu.SemaphoreType.DMA((4,)),
            pltpu.SemaphoreType.DMA((32,)),
        ],
        compiler_params=pltpu.CompilerParams(vmem_limit_bytes=60 << 20),
        name="open_leaves",
    )(ids, leaf_pos, leaf_mass)


def local_kernel(
    eg_ref, ec_ref, pos_ref, node_ref, mass_ref, list_ref, acc_ref, todo_ref, ynt, xk, raw
):
    peers = ec_ref.shape[0]

    def enlist(p, count):
        for s in range(SLOTS):
            todo_ref[count + s] = (p * SLOTS + s) * 256 + eg_ref[s, p]
        return count + ec_ref[p]

    count = lax.fori_loop(0, peers, enlist, 0)
    for s in range(BATCH):
        todo_ref[count + s] = 0
    todo_ref[todo_ref.shape[0] - 1] = count

    nodes = node_ref.shape[1]
    y = [node_ref[c : c + 1, :] - MID for c in range(3)]
    mass = mass_ref[...]
    yk = jnp.concatenate(source_rows(y, 1.0) + [jnp.zeros((8, nodes), f32)], axis=0)
    ynt[...] = jnp.transpose(yk).astype(bf16)
    tab = jnp.concatenate([mass * y[0], mass * y[1], mass * y[2], mass], axis=0)
    tab = jnp.concatenate([tab, tab], axis=0)
    xk[...] = jnp.zeros_like(xk)
    row128 = lax.broadcasted_iota(jnp.int32, (LANES, nodes), 0)
    row16 = lax.broadcasted_iota(jnp.int32, (16, nodes), 0)
    upper = lax.broadcasted_iota(jnp.int32, (8, LANES), 0) < 4
    raw[...] = jnp.zeros_like(raw)

    def one_block(b, carry):
        first = pl.multiple_of(b * TOGETHER, TOGETHER)
        places = []
        for q in range(TOGETHER // 8):
            x = [pos_ref[c, pl.ds(first + q * 8, 8), :] - MID for c in range(3)]
            places.append(x)
            for r, v in enumerate(target_rows(x)):
                xk[pl.ds(q * 8 * ROWS + r, 8, stride=ROWS), :] = v
        lists = list_ref[pl.ds(first, TOGETHER), :]
        counts = []
        for g in range(TOGETHER):
            wanted = lists[g : g + 1, :]
            low = jnp.where(row128 == (wanted & 127), 1.0, 0.0).astype(bf16)
            high = jnp.where(row16 == (wanted >> 7), 1.0, 0.0).astype(bf16)
            counts.append(dot_t(high, low))
        for p in range(TOGETHER // 2):
            parts = []
            for h in range(nodes // LANES):
                both = jnp.where(
                    upper, counts[2 * p][h : h + 1, :], counts[2 * p + 1][h : h + 1, :]
                )
                parts.append(tab[:, h * LANES : (h + 1) * LANES] * both)
            a, d, e = split3(jnp.concatenate(parts, axis=1))
            weights = jnp.concatenate([a, d, e, jnp.zeros_like(a)], axis=0).astype(bf16)
            xa = xk[pl.ds(2 * p * ROWS, ROWS), :]
            xb = xk[pl.ds((2 * p + 1) * ROWS, ROWS), :]
            rhs = jnp.concatenate([xa, xb], axis=1).astype(bf16)
            total = jnp.zeros((32, 2 * LANES), f32)
            for h in range(nodes // 256):
                his, los = [], []
                for k in range(256 // 128):
                    rows = pl.ds(h * 256 + k * 128, 128)
                    a, d = split2(inv_cube(dot(ynt[rows, :], rhs)))
                    his.append(a)
                    los.append(d)
                part = weights[:, h * 256 : (h + 1) * 256]
                total = total + dot(part, jnp.concatenate(his, axis=0)) + dot(part, jnp.concatenate(los, axis=0))
            total = total[0:8] + total[8:16] + total[16:24]
            raw[pl.ds(2 * p * 8, 4), :] = total[0:4, :LANES]
            raw[pl.ds((2 * p + 1) * 8, 4), :] = total[4:8, LANES:]
        for q, x in enumerate(places):
            weight = raw[pl.ds(q * 64 + 3, 8, stride=8), :]
            for c in range(3):
                pull = raw[pl.ds(q * 64 + c, 8, stride=8), :] - x[c] * weight
                acc_ref[c, pl.ds(first + q * 8, 8), :] = pull
        return carry

    lax.fori_loop(0, acc_ref.shape[1] // TOGETHER, one_block, 0)


def local_pull(export_group, export_count, pos, node_pos, node_mass, lists):
    groups = pos.shape[1]
    nodes = node_pos.shape[1]
    entries = export_group.shape[0] * export_group.shape[1] + 2 * BATCH
    pairs = groups * LANES * nodes
    return pl.pallas_call(
        local_kernel,
        out_shape=(
            jax.ShapeDtypeStruct((3, groups, LANES), f32),
            jax.ShapeDtypeStruct((entries,), jnp.int32),
        ),
        in_specs=[SMEM_SPEC] * 2 + [VMEM_SPEC] * 4,
        out_specs=[VMEM_SPEC, SMEM_SPEC],
        scratch_shapes=[
            pltpu.VMEM((nodes, ROWS), bf16),
            pltpu.VMEM((TOGETHER * ROWS, LANES), f32),
            pltpu.VMEM((TOGETHER * 8, LANES), f32),
        ],
        compiler_params=pltpu.CompilerParams(vmem_limit_bytes=16 << 20),
        cost_estimate=pl.CostEstimate(
            flops=pairs * 2000, bytes_accessed=4 << 20, transcendentals=pairs
        ),
        name="local_pull",
    )(export_group, export_count, pos, node_pos, node_mass, lists)


def remote_kernel(
    todo_ref, recv_ref, pos_ref, vel_ref, local_ref, out_ref, todo, tile, place, xk, yk, tk, acc, sem
):
    groups = pos_ref.shape[1]
    fetch = pltpu.make_async_copy(todo_ref, todo, sem)
    fetch.start()
    blank = jnp.zeros((8, LANES), f32)
    for s in range(BATCH):
        xk[pl.ds(s * ROWS + 24, 8), :] = blank
    for s in range(2 * BATCH):
        yk[pl.ds(s * ROWS + 24, 8), :] = blank
        tk[pl.ds(s * 16 + 8, 8), :] = blank

    def clear(i, carry):
        acc[pl.ds(pl.multiple_of(i * 64, 64), 64), :] = jnp.zeros((64, LANES), f32)
        return carry

    lax.fori_loop(0, groups * 8 // 64, clear, 0)
    fetch.wait()
    count = todo[todo.shape[0] - 1]
    lane = lax.broadcasted_iota(jnp.int32, (8, LANES), 1).astype(f32)
    scale = 1.0 + lane * (1.0 / LANES)
    lift = scale * jnp.sqrt(scale)

    def one_batch(size, start, b, carry):
        owners = []
        for s in range(size):
            entry = todo[start + b * size + s]
            g = entry & 255
            owners.append(g)
            tile[pl.ds(s * 8, 8), :] = recv_ref[pl.ds(pl.multiple_of((entry >> 8) * 8, 8), 8), :]
            for c in range(3):
                place[c, pl.ds(s, 1), :] = pos_ref[c, pl.ds(g, 1), :]
        for q in range(size // 8):
            first = q * 8
            rank = lax.broadcasted_iota(jnp.int32, (8, LANES), 0) + (start + b * size + first)
            x = [place[c, pl.ds(first, 8), :] - MID for c in range(3)]
            for r, v in enumerate(target_rows(x)):
                xk[pl.ds(first * ROWS + r, 8, stride=ROWS), :] = v
            for h in range(2):
                y = [tile[pl.ds(first * 8 + 4 * h + c, 8, stride=8), :] - MID for c in range(3)]
                m = tile[pl.ds(first * 8 + 4 * h + 3, 8, stride=8), :]
                m = jnp.where(rank < count, m * lift, 0.0)
                base = h * BATCH + first
                for r, v in enumerate(source_rows(y, scale)):
                    yk[pl.ds(base * ROWS + r, 8, stride=ROWS), :] = v
                for c, v in enumerate([m * y[0], m * y[1], m * y[2], m]):
                    for j, part in enumerate(split3(v)):
                        tk[pl.ds(base * 16 + 4 * j + c, 8, stride=16), :] = part
        for s in range(size):
            xt = jnp.transpose(xk[pl.ds(s * ROWS, ROWS), :]).astype(bf16)
            rhs = [yk[pl.ds((h * BATCH + s) * ROWS, ROWS), :] for h in range(2)]
            r2 = dot(xt, jnp.concatenate(rhs, axis=1).astype(bf16))
            part = [tk[pl.ds((h * BATCH + s) * 16, 16), :] for h in range(2)]
            part = jnp.concatenate(part, axis=1).astype(bf16)
            total = dot_t(part, inv_cube(r2).astype(bf16))
            rows = pl.ds(pl.multiple_of(owners[s] * 8, 8), 8)
            acc[rows, :] += total[0:8] + total[8:16]
        return carry

    whole = count // BATCH
    lax.fori_loop(0, whole, functools.partial(one_batch, BATCH, 0), 0)
    rest = count - whole * BATCH
    lax.fori_loop(0, (rest + TAIL - 1) // TAIL, functools.partial(one_batch, TAIL, whole * BATCH), 0)

    def finish(b, carry):
        first = pl.multiple_of(b * 8, 8)
        rows = pl.ds(first, 8)
        total = []
        for c in range(4):
            v = acc[pl.ds(first * 8 + c, 8, stride=8), :]
            total.append(v + acc[pl.ds(first * 8 + 4 + c, 8, stride=8), :])
        for c in range(3):
            x = pos_ref[c, rows, :]
            pull = local_ref[c, rows, :] + total[c] - (x - MID) * total[3]
            out_ref[c, rows, :] = x
            out_ref[3 + c, rows, :] = vel_ref[c, rows, :] + KICK * pull
        return carry

    lax.fori_loop(0, groups // 8, finish, 0, unroll=2)


def remote_pull(todo, recv, pos, vel, local_acc):
    groups = pos.shape[1]
    return pl.pallas_call(
        remote_kernel,
        out_shape=jax.ShapeDtypeStruct((6, groups, LANES), f32),
        in_specs=[pl.BlockSpec(memory_space=pl.ANY)] + [VMEM_SPEC] * 4,
        out_specs=VMEM_SPEC,
        scratch_shapes=[
            pltpu.SMEM(todo.shape, jnp.int32),
            pltpu.VMEM((BATCH * 8, LANES), f32),
            pltpu.VMEM((3, BATCH, LANES), f32),
            pltpu.VMEM((BATCH * ROWS, LANES), f32),
            pltpu.VMEM((2 * BATCH * ROWS, LANES), f32),
            pltpu.VMEM((2 * BATCH * 16, LANES), f32),
            pltpu.VMEM((groups * 8, LANES), f32),
            pltpu.SemaphoreType.DMA,
        ],
        compiler_params=pltpu.CompilerParams(vmem_limit_bytes=24 << 20),
        name="remote_pull",
    )(todo, recv, pos, vel, local_acc)


def shifted(value, axis, steps):
    count = lax.axis_size(axis)
    return lax.ppermute(value, axis, [(source, source + steps) for source in range(count - steps)])


def per_device(
    group_pos,
    group_vel,
    leaf_pos,
    leaf_mass,
    node_pos,
    node_mass,
    group_nodes,
    export_group,
    export_leaf,
    export_count,
    move_count,
):
    peers = export_group.shape[1]
    groups = group_pos.shape[0]
    asked = jnp.concatenate(
        [export_leaf[0].reshape(peers, 16), jnp.broadcast_to(move_count[:, None], (peers, 1))], axis=1
    )
    got = lax.all_to_all(asked, AXES, split_axis=0, concat_axis=0, tiled=True)
    pos = jnp.transpose(group_pos, (1, 0, 2))
    vel = jnp.transpose(group_vel, (1, 0, 2))
    mass = node_mass[None, :]
    exported = jnp.transpose(export_group[0])
    opened = open_leaves(got, jnp.transpose(leaf_pos, (1, 0, 2)), leaf_mass)
    opened, mass = lax.optimization_barrier((opened, mass))
    recv = lax.all_to_all(opened, AXES, split_axis=0, concat_axis=0, tiled=True)
    local_acc, todo = local_pull(exported, export_count[0], pos, node_pos, mass, group_nodes)
    kicked = remote_pull(todo, recv.reshape(-1, LANES), pos, vel, local_acc)
    me = lax.axis_index(AXES)
    before = jnp.where(me > 0, got[jnp.maximum(me - 1, 0), 16], 0)
    leaving = move_count[0]
    arrived = shifted(kicked[:, groups - MOVE_MAX :], AXES, 1)
    keep = (jnp.arange(groups) < groups - leaving).astype(f32)
    stacked = jnp.concatenate(
        [arrived, kicked * keep[None, :, None], jnp.zeros((6, MOVE_MAX, LANES), f32)], axis=1
    )
    moved = lax.dynamic_slice_in_dim(stacked, MOVE_MAX - before, groups + MOVE_MAX, 1)
    return jnp.transpose(moved, (1, 0, 2))


def solution(mesh):
    in_specs = (
        P(AXES, None, None),
        P(AXES, None, None),
        P(AXES, None, None),
        P(AXES, None),
        P(None, AXES),
        P(AXES),
        P(AXES, None),
        P(AXES, None, None),
        P(AXES, None, None, None),
        P(AXES, None),
        P(AXES),
    )
    return jax.shard_map(
        per_device,
        mesh=mesh,
        in_specs=in_specs,
        out_specs=P(AXES, None, None),
        check_vma=False,
    )
```

```python
import functools

import jax
import jax.numpy as jnp
from jax import lax
from jax.experimental import pallas as pl
from jax.experimental.pallas import tpu as pltpu
from jax.sharding import PartitionSpec as P

AXES = ("dom", "bulk")
MOVE_MAX = 16
SOFT_SQ = 0.001
KICK = 0.5
MID = 0.5
LANES = 128
ROWS = 32
SLOTS = 8
TOGETHER = 32
BATCH = 64
TAIL = 16

SMEM_SPEC = pl.BlockSpec(memory_space=pltpu.SMEM)
VMEM_SPEC = pl.BlockSpec(memory_space=pltpu.VMEM)

f32 = jnp.float32
bf16 = jnp.bfloat16


def dot(a, b):
    return lax.dot_general(a, b, (((1,), (0,)), ((), ())), preferred_element_type=f32)


def dot_t(a, b):
    return lax.dot_general(a, b, (((1,), (1,)), ((), ())), preferred_element_type=f32)


def split3(v):
    a = v.astype(bf16).astype(f32)
    r = v - a
    b = r.astype(bf16).astype(f32)
    return a, b, r - b


def split2(w):
    hi = w.astype(bf16)
    return hi, (w - hi.astype(f32)).astype(bf16)


def target_rows(x):
    rows = []
    for c in range(3):
        a, b, d = split3(x[c])
        rows += [a, a, b, b, a, d]
    rows += list(split3(x[0] * x[0] + x[1] * x[1] + x[2] * x[2]))
    one = jnp.ones_like(x[0])
    return rows + [one, one, one]


def source_rows(y, scale):
    rows = []
    for c in range(3):
        a, b, d = split3(y[c] * (-2.0 * scale))
        rows += [a, b, a, b, d, a]
    one = jnp.ones_like(y[0]) * scale
    rows += [one, one, one]
    rows += list(split3((y[0] * y[0] + y[1] * y[1] + y[2] * y[2] + SOFT_SQ) * scale))
    return rows


def inv_cube(r2):
    rs = lax.rsqrt(r2)
    return rs * rs * rs


def open_kernel(
    ids_any, pos_hbm, mass_hbm, out_hbm, ids_ref, pos, mass, table, out, ids_sem, in_sem, out_sem
):
    fetch = pltpu.make_async_copy(ids_any, ids_ref, ids_sem)
    fetch.start()
    leaf_count = pos.shape[1]
    peers = out.shape[0]
    loads = []
    part = leaf_count // 1
    for q in range(1):
        rows = pl.ds(q * part, part)
        loads.append(pltpu.make_async_copy(mass_hbm.at[rows], mass.at[rows], in_sem.at[4 * q + 3]))
        for c in range(3):
            loads.append(pltpu.make_async_copy(pos_hbm.at[c, rows], pos.at[c, rows], in_sem.at[4 * q + c]))
    for load in loads:
        load.start()
    for load in loads:
        load.wait()

    def build(b, carry):
        first = pl.multiple_of(b * 8, 8)
        for c in range(4):
            v = pos[c, pl.ds(first, 8), :] if c < 3 else mass[pl.ds(first, 8), :]
            table[pl.ds(first * 8 + c, 8, stride=8), :] = v
            table[pl.ds(first * 8 + 4 + c, 8, stride=8), :] = v
        return carry

    lax.fori_loop(0, leaf_count // 8, build, 0, unroll=8)
    upper = lax.broadcasted_iota(jnp.int32, (8, LANES), 0) < 4

    def one_peer(p, carry):
        for s in range(SLOTS):
            i0 = pl.multiple_of(ids_ref[p, 2 * s] * 8, 8)
            i1 = pl.multiple_of(ids_ref[p, 2 * s + 1] * 8, 8)
            out[p, pl.ds(s * 8, 8), :] = jnp.where(
                upper, table[pl.ds(i0, 8), :], table[pl.ds(i1, 8), :]
            )
        return carry

    fetch.wait()
    stores = []
    step = peers // 32
    for q in range(32):
        lax.fori_loop(q * step, (q + 1) * step, one_peer, 0, unroll=4)
        rows = pl.ds(q * step, step)
        stores.append(pltpu.make_async_copy(out.at[rows], out_hbm.at[rows], out_sem.at[q]))
        stores[-1].start()
    for store in stores:
        store.wait()


def open_leaves(ids, leaf_pos, leaf_mass):
    peers = ids.shape[0]
    shape = (peers, SLOTS * 8, LANES)
    return pl.pallas_call(
        open_kernel,
        out_shape=jax.ShapeDtypeStruct(shape, f32),
        in_specs=[
            pl.BlockSpec(memory_space=pl.ANY),
            pl.BlockSpec(memory_space=pltpu.HBM),
            pl.BlockSpec(memory_space=pltpu.HBM),
        ],
        out_specs=pl.BlockSpec(memory_space=pltpu.HBM),
        scratch_shapes=[
            pltpu.SMEM(ids.shape, jnp.int32),
            pltpu.VMEM(leaf_pos.shape, f32),
            pltpu.VMEM(leaf_mass.shape, f32),
            pltpu.VMEM((leaf_pos.shape[1] * 8, LANES), f32),
            pltpu.VMEM(shape, f32),
            pltpu.SemaphoreType.DMA,
            pltpu.SemaphoreType.DMA((4,)),
            pltpu.SemaphoreType.DMA((32,)),
        ],
        compiler_params=pltpu.CompilerParams(vmem_limit_bytes=60 << 20),
        name="open_leaves",
    )(ids, leaf_pos, leaf_mass)


def local_kernel(
    eg_ref, ec_ref, pos_ref, node_ref, mass_ref, list_ref, acc_ref, todo_ref, ynt, xk, raw
):
    peers = ec_ref.shape[0]

    def enlist(p, count):
        for s in range(SLOTS):
            todo_ref[count + s] = (p * SLOTS + s) * 256 + eg_ref[s, p]
        return count + ec_ref[p]

    count = lax.fori_loop(0, peers, enlist, 0)
    for s in range(BATCH):
        todo_ref[count + s] = 0
    todo_ref[todo_ref.shape[0] - 1] = count

    nodes = node_ref.shape[1]
    y = [node_ref[c : c + 1, :] - MID for c in range(3)]
    mass = mass_ref[...]
    yk = jnp.concatenate(source_rows(y, 1.0) + [jnp.zeros((8, nodes), f32)], axis=0)
    ynt[...] = jnp.transpose(yk).astype(bf16)
    tab = jnp.concatenate([mass * y[0], mass * y[1], mass * y[2], mass], axis=0)
    tab = jnp.concatenate([tab, tab], axis=0)
    xk[...] = jnp.zeros_like(xk)
    row128 = lax.broadcasted_iota(jnp.int32, (LANES, nodes), 0)
    row16 = lax.broadcasted_iota(jnp.int32, (16, nodes), 0)
    upper = lax.broadcasted_iota(jnp.int32, (8, LANES), 0) < 4
    raw[...] = jnp.zeros_like(raw)

    def one_block(b, carry):
        first = pl.multiple_of(b * TOGETHER, TOGETHER)
        places = []
        for q in range(TOGETHER // 8):
            x = [pos_ref[c, pl.ds(first + q * 8, 8), :] - MID for c in range(3)]
            places.append(x)
            for r, v in enumerate(target_rows(x)):
                xk[pl.ds(q * 8 * ROWS + r, 8, stride=ROWS), :] = v
        lists = list_ref[pl.ds(first, TOGETHER), :]
        counts = []
        for g in range(TOGETHER):
            wanted = lists[g : g + 1, :]
            low = jnp.where(row128 == (wanted & 127), 1.0, 0.0).astype(bf16)
            high = jnp.where(row16 == (wanted >> 7), 1.0, 0.0).astype(bf16)
            counts.append(dot_t(high, low))
        for p in range(TOGETHER // 2):
            parts = []
            for h in range(nodes // LANES):
                both = jnp.where(
                    upper, counts[2 * p][h : h + 1, :], counts[2 * p + 1][h : h + 1, :]
                )
                parts.append(tab[:, h * LANES : (h + 1) * LANES] * both)
            a, d, e = split3(jnp.concatenate(parts, axis=1))
            weights = jnp.concatenate([a, d, e, jnp.zeros_like(a)], axis=0).astype(bf16)
            xa = xk[pl.ds(2 * p * ROWS, ROWS), :]
            xb = xk[pl.ds((2 * p + 1) * ROWS, ROWS), :]
            rhs = jnp.concatenate([xa, xb], axis=1).astype(bf16)
            total = jnp.zeros((32, 2 * LANES), f32)
            for h in range(nodes // 256):
                his, los = [], []
                for k in range(256 // 128):
                    rows = pl.ds(h * 256 + k * 128, 128)
                    a, d = split2(inv_cube(dot(ynt[rows, :], rhs)))
                    his.append(a)
                    los.append(d)
                part = weights[:, h * 256 : (h + 1) * 256]
                total = total + dot(part, jnp.concatenate(his, axis=0)) + dot(part, jnp.concatenate(los, axis=0))
            total = total[0:8] + total[8:16] + total[16:24]
            raw[pl.ds(2 * p * 8, 4), :] = total[0:4, :LANES]
            raw[pl.ds((2 * p + 1) * 8, 4), :] = total[4:8, LANES:]
        for q, x in enumerate(places):
            weight = raw[pl.ds(q * 64 + 3, 8, stride=8), :]
            for c in range(3):
                pull = raw[pl.ds(q * 64 + c, 8, stride=8), :] - x[c] * weight
                acc_ref[c, pl.ds(first + q * 8, 8), :] = pull
        return carry

    lax.fori_loop(0, acc_ref.shape[1] // TOGETHER, one_block, 0)


def local_pull(export_group, export_count, pos, node_pos, node_mass, lists):
    groups = pos.shape[1]
    nodes = node_pos.shape[1]
    entries = export_group.shape[0] * export_group.shape[1] + 2 * BATCH
    pairs = groups * LANES * nodes
    return pl.pallas_call(
        local_kernel,
        out_shape=(
            jax.ShapeDtypeStruct((3, groups, LANES), f32),
            jax.ShapeDtypeStruct((entries,), jnp.int32),
        ),
        in_specs=[SMEM_SPEC] * 2 + [VMEM_SPEC] * 4,
        out_specs=[VMEM_SPEC, SMEM_SPEC],
        scratch_shapes=[
            pltpu.VMEM((nodes, ROWS), bf16),
            pltpu.VMEM((TOGETHER * ROWS, LANES), f32),
            pltpu.VMEM((TOGETHER * 8, LANES), f32),
        ],
        compiler_params=pltpu.CompilerParams(vmem_limit_bytes=16 << 20),
        cost_estimate=pl.CostEstimate(
            flops=pairs * 2000, bytes_accessed=4 << 20, transcendentals=pairs
        ),
        name="local_pull",
    )(export_group, export_count, pos, node_pos, node_mass, lists)


def remote_kernel(
    todo_ref, recv_ref, pos_ref, vel_ref, local_ref, out_ref, todo, tile, place, xk, yk, tk, acc, sem
):
    groups = pos_ref.shape[1]
    fetch = pltpu.make_async_copy(todo_ref, todo, sem)
    fetch.start()
    blank = jnp.zeros((8, LANES), f32)
    for s in range(BATCH):
        xk[pl.ds(s * ROWS + 24, 8), :] = blank
    for s in range(2 * BATCH):
        yk[pl.ds(s * ROWS + 24, 8), :] = blank
        tk[pl.ds(s * 16 + 8, 8), :] = blank

    def clear(i, carry):
        acc[pl.ds(pl.multiple_of(i * 64, 64), 64), :] = jnp.zeros((64, LANES), f32)
        return carry

    lax.fori_loop(0, groups * 8 // 64, clear, 0, unroll=4)
    fetch.wait()
    count = todo[todo.shape[0] - 1]
    lane = lax.broadcasted_iota(jnp.int32, (8, LANES), 1).astype(f32)
    scale = 1.0 + lane * (1.0 / LANES)
    lift = scale * jnp.sqrt(scale)

    def one_batch(size, start, b, carry):
        owners = []
        for s in range(size):
            entry = todo[start + b * size + s]
            g = entry & 255
            owners.append(g)
            tile[pl.ds(s * 8, 8), :] = recv_ref[pl.ds(pl.multiple_of((entry >> 8) * 8, 8), 8), :]
            for c in range(3):
                place[c, pl.ds(s, 1), :] = pos_ref[c, pl.ds(g, 1), :]
        for q in range(size // 8):
            first = q * 8
            rank = lax.broadcasted_iota(jnp.int32, (8, LANES), 0) + (start + b * size + first)
            x = [place[c, pl.ds(first, 8), :] - MID for c in range(3)]
            for r, v in enumerate(target_rows(x)):
                xk[pl.ds(first * ROWS + r, 8, stride=ROWS), :] = v
            for h in range(2):
                y = [tile[pl.ds(first * 8 + 4 * h + c, 8, stride=8), :] - MID for c in range(3)]
                m = tile[pl.ds(first * 8 + 4 * h + 3, 8, stride=8), :]
                m = jnp.where(rank < count, m * lift, 0.0)
                base = h * BATCH + first
                for r, v in enumerate(source_rows(y, scale)):
                    yk[pl.ds(base * ROWS + r, 8, stride=ROWS), :] = v
                for c, v in enumerate([m * y[0], m * y[1], m * y[2], m]):
                    for j, part in enumerate(split3(v)):
                        tk[pl.ds(base * 16 + 4 * j + c, 8, stride=16), :] = part
        for s in range(size):
            xt = jnp.transpose(xk[pl.ds(s * ROWS, ROWS), :]).astype(bf16)
            rhs = [yk[pl.ds((h * BATCH + s) * ROWS, ROWS), :] for h in range(2)]
            r2 = dot(xt, jnp.concatenate(rhs, axis=1).astype(bf16))
            part = [tk[pl.ds((h * BATCH + s) * 16, 16), :] for h in range(2)]
            part = jnp.concatenate(part, axis=1).astype(bf16)
            total = dot_t(part, inv_cube(r2).astype(bf16))
            rows = pl.ds(pl.multiple_of(owners[s] * 8, 8), 8)
            acc[rows, :] += total[0:8] + total[8:16]
        return carry

    whole = count // BATCH
    lax.fori_loop(0, whole, functools.partial(one_batch, BATCH, 0), 0)
    rest = count - whole * BATCH
    lax.fori_loop(0, (rest + TAIL - 1) // TAIL, functools.partial(one_batch, TAIL, whole * BATCH), 0)

    def finish(b, carry):
        first = pl.multiple_of(b * 8, 8)
        rows = pl.ds(first, 8)
        total = []
        for c in range(4):
            v = acc[pl.ds(first * 8 + c, 8, stride=8), :]
            total.append(v + acc[pl.ds(first * 8 + 4 + c, 8, stride=8), :])
        for c in range(3):
            x = pos_ref[c, rows, :]
            pull = local_ref[c, rows, :] + total[c] - (x - MID) * total[3]
            out_ref[c, rows, :] = x
            out_ref[3 + c, rows, :] = vel_ref[c, rows, :] + KICK * pull
        return carry

    lax.fori_loop(0, groups // 8, finish, 0, unroll=8)


def remote_pull(todo, recv, pos, vel, local_acc):
    groups = pos.shape[1]
    return pl.pallas_call(
        remote_kernel,
        out_shape=jax.ShapeDtypeStruct((6, groups, LANES), f32),
        in_specs=[pl.BlockSpec(memory_space=pl.ANY)] + [VMEM_SPEC] * 4,
        out_specs=VMEM_SPEC,
        scratch_shapes=[
            pltpu.SMEM(todo.shape, jnp.int32),
            pltpu.VMEM((BATCH * 8, LANES), f32),
            pltpu.VMEM((3, BATCH, LANES), f32),
            pltpu.VMEM((BATCH * ROWS, LANES), f32),
            pltpu.VMEM((2 * BATCH * ROWS, LANES), f32),
            pltpu.VMEM((2 * BATCH * 16, LANES), f32),
            pltpu.VMEM((groups * 8, LANES), f32),
            pltpu.SemaphoreType.DMA,
        ],
        compiler_params=pltpu.CompilerParams(vmem_limit_bytes=24 << 20),
        name="remote_pull",
    )(todo, recv, pos, vel, local_acc)


def shifted(value, axis, steps):
    count = lax.axis_size(axis)
    return lax.ppermute(value, axis, [(source, source + steps) for source in range(count - steps)])


def per_device(
    group_pos,
    group_vel,
    leaf_pos,
    leaf_mass,
    node_pos,
    node_mass,
    group_nodes,
    export_group,
    export_leaf,
    export_count,
    move_count,
):
    peers = export_group.shape[1]
    groups = group_pos.shape[0]
    asked = jnp.concatenate(
        [export_leaf[0].reshape(peers, 16), jnp.broadcast_to(move_count[:, None], (peers, 1))], axis=1
    )
    got = lax.all_to_all(asked, AXES, split_axis=0, concat_axis=0, tiled=True)
    pos = jnp.transpose(group_pos, (1, 0, 2))
    vel = jnp.transpose(group_vel, (1, 0, 2))
    mass = node_mass[None, :]
    exported = jnp.transpose(export_group[0])
    opened = open_leaves(got, jnp.transpose(leaf_pos, (1, 0, 2)), leaf_mass)
    opened, mass = lax.optimization_barrier((opened, mass))
    recv = lax.all_to_all(opened, AXES, split_axis=0, concat_axis=0, tiled=True)
    local_acc, todo = local_pull(exported, export_count[0], pos, node_pos, mass, group_nodes)
    kicked = remote_pull(todo, recv.reshape(-1, LANES), pos, vel, local_acc)
    me = lax.axis_index(AXES)
    before = jnp.where(me > 0, got[jnp.maximum(me - 1, 0), 16], 0)
    leaving = move_count[0]
    arrived = shifted(kicked[:, groups - MOVE_MAX :], AXES, 1)
    keep = (jnp.arange(groups) < groups - leaving).astype(f32)
    stacked = jnp.concatenate(
        [arrived, kicked * keep[None, :, None], jnp.zeros((6, MOVE_MAX, LANES), f32)], axis=1
    )
    moved = lax.dynamic_slice_in_dim(stacked, MOVE_MAX - before, groups + MOVE_MAX, 1)
    return jnp.transpose(moved, (1, 0, 2))


def solution(mesh):
    in_specs = (
        P(AXES, None, None),
        P(AXES, None, None),
        P(AXES, None, None),
        P(AXES, None),
        P(None, AXES),
        P(AXES),
        P(AXES, None),
        P(AXES, None, None),
        P(AXES, None, None, None),
        P(AXES, None),
        P(AXES),
    )
    return jax.shard_map(
        per_device,
        mesh=mesh,
        in_specs=in_specs,
        out_specs=P(AXES, None, None),
        check_vma=False,
    )
```
